512 devices in a mesh: rep: 8 (over y, core), exp: 64 (over x, z).
Axes of the slice: x: 4, y: 4, z: 16, core: 2. Of those that a mesh axis runs over, the one named last changes fastest.
Arguments:
- grad_out: bfloat16 [65536, 2048], P(('rep', 'exp')), may hold values from -6 to 6
- expert_ids: int32 [65536, 8], P(('rep', 'exp')), may hold values from 0 to 63, all different within a row; in each aligned block of 128 rows (0 to 127, 128 to 255, ...) at most 20 rows name the same one
- gates: float32 [65536, 8], P(('rep', 'exp')), may hold values from 0.02 to 0.5
- hidden: bfloat16 [8, 64, 1280, 768], P('rep', 'exp'), may hold values from -6 to 6
- w_down: bfloat16 [64, 768, 2048], P('exp', 'rep'), may hold values from -0.21875 to 0.21875
- q_start: float32 [64, 2048, 32], P('exp'), may hold values from -6 to 6
Outputs:
- grad_hidden: bfloat16 [65536, 8, 768], P(('rep', 'exp'))
- p_basis: float32 [64, 768, 32], P('exp')
- q_factor: float32 [64, 2048, 32], P('exp')
The draws below stay inside these ranges and needn't reach their ends.
Inputs may be any that keep to these rules, and one draw needn't show every extreme that they name: `expert_ids`: within the 128 rows of one device no expert is named more than 20 times, a bound that some block reaches.
All inputs are finite; a program needn't handle non-finite values.
Results may differ from the reference program's by a relative error of at most 0.0049.
Values may be sent and summed in bfloat16 or wider, within the bound.
No kernel may reach another device: no remote copies, remote signals or barrier semaphores. Data moves between devices by JAX's collectives and lax.ppermute only.
A program may use at most 128 MiB of HBM per device.

```python
import math
import jax
import jax.numpy as jnp
import numpy as np
from jax import lax

D = 2048
FF = 768
TOPK = 8
RANK = 32
TOK_DEV = 128
EXPERTS = 64
CAP = 20
SLOTS = 1280
TOKENS = 65536
N_REP = 8
N_EXP = 64


def shard_levels(key, shape, shards, smallest, largest):
    def one(dim, shards_of):
        draws = jax.random.uniform(jax.random.fold_in(jax.random.fold_in(key, 6), dim), (shards_of,), jnp.float32, smallest / len(shards), largest / len(shards))
        return jnp.repeat(jnp.exp(draws), shape[dim] // shards_of).reshape((-1,) + (1,) * (len(shape) - dim - 1))

    factor_of = one(*shards[0])
    for cut in shards[1:]:
        factor_of = factor_of * one(*cut)
    return factor_of


def deal_out(key, own, number, rows, number_of, top, bound, slope):
    ranking = jax.random.permutation(key, number_of)
    heavy_load, common = portions_of(number_of, rows * top, bound, slope, True), portions_of(number_of, rows * top, bound, slope, False)
    places = jnp.arange(number_of)

    def named(tallies, offset_by):
        used = int((tallies > 0).sum())
        fixed = max(1, used // 4)
        moved = fixed + (places - fixed + offset_by * (used - fixed)) % max(1, number_of - fixed)
        return jnp.zeros((number_of,), jnp.int32).at[ranking[jnp.where(places < fixed, places, moved)]].set(jnp.asarray(tallies, jnp.int32))

    tallies = jnp.where(number % 4 == 0, named(heavy_load, number // 4), named(common, number - number // 4 - 1))
    mixed = jax.random.permutation(jax.random.fold_in(own, 3), number_of)
    source_of, sink = mixed[0:number_of // 2 * 2:2], mixed[1:number_of // 2 * 2:2]
    slack = jnp.minimum(tallies[source_of] - 1, bound - tallies[sink]) // 2
    slack = jnp.where((source_of == ranking[0]) | (sink == ranking[0]) | (tallies[sink] == 0), 0, jnp.maximum(slack, 0))
    moved = jax.random.randint(jax.random.fold_in(own, 4), (number_of // 2,), 0, 1 << 20) % (slack + 1)
    tallies = tallies.at[source_of].add(-moved).at[sink].add(moved)
    members = jnp.searchsorted(jnp.cumsum(tallies), jnp.arange(rows * top), side="right").astype(jnp.int32)
    listing = members.reshape(top, rows).T
    listing = listing[jax.random.permutation(jax.random.fold_in(own, 1), rows)]
    offset_by = jax.random.randint(jax.random.fold_in(own, 2), (rows, 1), 0, top)
    return jnp.take_along_axis(listing, (jnp.arange(top)[None, :] + offset_by) % top, axis=1)


def portions_of(amount, total, reach, skew, full):
    weights = [(1 << 20) // math.isqrt(grade ** skew) + 1 for grade in range(1, amount + 1)]
    largest = reach if full else min(reach, max(-(-total // amount), total * weights[0] // sum(weights)))
    least = 1 if total - largest >= amount - 1 else 0
    counts, surplus = [largest] + [least] * (amount - 1), total - largest - least * (amount - 1)
    while surplus > 0:
        candidates = [i for i in range(1, amount) if counts[i] < largest] or [i for i in range(1, amount) if counts[i] < reach]
        pool, remaining = sum([weights[i] for i in candidates]), surplus
        for i in candidates:
            extra = min(reach - counts[i], max(1, remaining * weights[i] // pool), surplus)
            counts[i] = counts[i] + extra
            surplus = surplus - extra
    return np.array(counts)


def centred(rng, dims, deviation, limit, pieces=(), held_as=jnp.bfloat16):
    factor_of = shard_levels(rng, dims, pieces, -0.22, 0.18) if pieces else 1.0
    drawn = jax.random.normal(rng, dims, jnp.float32) * deviation * factor_of
    return jnp.minimum(jnp.maximum(drawn, -limit), limit).astype(held_as)


def setup_inputs(seed: int = 0) -> dict:
    splits = jax.random.split(jax.random.key(seed), 7)
    grad_out = centred(splits[0], (TOKENS, D), 1.0, 6.0, ((0, 512),))
    expert_ids_keys = jax.random.split(jax.random.fold_in(splits[1], 1), TOKENS // TOK_DEV)
    expert_ids_turns = jax.random.permutation(jax.random.fold_in(splits[1], 3), TOKENS // TOK_DEV)
    expert_ids = jax.vmap(lambda own, number: deal_out(jax.random.fold_in(splits[1], 2), own, number, TOK_DEV, EXPERTS, TOPK, CAP, 2))(expert_ids_keys, expert_ids_turns).reshape((TOKENS, TOPK))
    gates = jnp.clip(jnp.exp(math.log(0.5) - 3.218876 * jax.random.uniform(splits[2], (TOKENS, TOPK), jnp.float32) ** shard_levels(splits[2], (TOKENS, TOPK), ((0, 512),), -0.2, 0.2)), 0.02, 0.5)
    hidden = centred(splits[3], (N_REP, EXPERTS, SLOTS, FF), 1.0, 6.0, ((0, 8), (1, 64)))
    w_down = centred(splits[4], (EXPERTS, FF, D), FF ** -0.5, 0.21875, ((0, 64), (1, 8)))
    q_start = centred(splits[5], (EXPERTS, D, RANK), 1.0, 6.0, ((0, 64),), jnp.float32)
    return dict(grad_out=grad_out, expert_ids=expert_ids, gates=gates, hidden=hidden, w_down=w_down, q_start=q_start)


def dispatch(grads_r, ids_r, gates_r):
    block_ids = ids_r.reshape(N_EXP, TOK_DEV * TOPK)
    onehot = (block_ids[:, :, None] == jnp.arange(EXPERTS, dtype=jnp.int32)[None, None, :]).astype(jnp.int32)
    before = (jnp.cumsum(onehot, axis=1) - 1).astype(jnp.int32)
    slots = lax.optimization_barrier(jnp.sum(onehot * before, axis=2)).astype(jnp.int32)
    scaled = (grads_r.astype(jnp.float32)[:, None, :] * gates_r[:, :, None]).astype(jnp.bfloat16)
    scaled = scaled.reshape(N_EXP, TOK_DEV * TOPK, D)
    source = jnp.broadcast_to(jnp.arange(N_EXP, dtype=jnp.int32)[:, None], block_ids.shape)
    buffer = jnp.zeros((EXPERTS, N_EXP, CAP, D), jnp.bfloat16).at[block_ids, source, slots].set(scaled)
    return (buffer.reshape(EXPERTS, SLOTS, D), block_ids, source, slots)

def orthonormal(p_sum):
    gram_matrix = jnp.dot(p_sum.T, p_sum, precision=lax.Precision.HIGHEST)
    factor = jnp.linalg.cholesky(gram_matrix)
    return jax.scipy.linalg.solve_triangular(factor, p_sum.T, lower=True).T

def reference(grad_out, expert_ids, gates, hidden, w_down, q_start):
    grads3 = grad_out.reshape(N_REP, N_EXP * TOK_DEV, D)
    ids3 = expert_ids.reshape(N_REP, N_EXP * TOK_DEV, TOPK)
    gates3 = gates.reshape(N_REP, N_EXP * TOK_DEV, TOPK)

    def first_pass(inputs):
        grads_r, ids_r, gates_r, hidden_r = inputs
        buffer, block_ids, source, slots = dispatch(grads_r, ids_r, gates_r)

        def per_expert(values):
            expert_rows, stored, weight, warm = values
            back_rows = jnp.dot(expert_rows.astype(jnp.float32), weight.T.astype(jnp.float32), preferred_element_type=jnp.float32).astype(jnp.bfloat16)
            projected = jnp.dot(expert_rows.astype(jnp.float32), warm, precision=lax.Precision.HIGHEST)
            p_part = jnp.dot(stored.astype(jnp.float32).T, projected, precision=lax.Precision.HIGHEST)
            return (back_rows, p_part)
        back_rows, p_part = lax.map(per_expert, (buffer, hidden_r, w_down, q_start))
        back_rows = back_rows.reshape(EXPERTS, N_EXP, CAP, FF)
        gathered = back_rows[block_ids, source, slots].reshape(N_EXP * TOK_DEV, TOPK, FF)
        return (gathered, p_part)
    grad_rows, p_parts = lax.map(first_pass, (grads3, ids3, gates3, hidden))
    p_sum = lax.optimization_barrier(jnp.sum(p_parts, axis=0))
    factor_basis = jax.vmap(orthonormal)(p_sum)

    def second_pass(inputs):
        grads_r, ids_r, gates_r, hidden_r = inputs
        buffer, block_ids, source, slots = dispatch(grads_r, ids_r, gates_r)

        def per_expert(values):
            expert_rows, stored, columns = values
            mapped = jnp.dot(stored.astype(jnp.float32), columns, precision=lax.Precision.HIGHEST)
            return jnp.dot(expert_rows.astype(jnp.float32).T, mapped, precision=lax.Precision.HIGHEST)
        return lax.map(per_expert, (buffer, hidden_r, factor_basis))
    q_parts = lax.map(second_pass, (grads3, ids3, gates3, hidden))
    q_factor = lax.optimization_barrier(jnp.sum(q_parts, axis=0)) / N_REP
    grad_hidden = grad_rows.reshape(TOKENS, TOPK, FF)
    return (grad_hidden, factor_basis * math.sqrt(FF), q_factor)
```

```python
import math

import jax
import jax.numpy as jnp
from jax import lax
from jax.experimental import pallas as pl
from jax.experimental.pallas import tpu as pltpu
from jax.sharding import Mesh
from jax.sharding import PartitionSpec as P

N_X = 4
N_Z = 16
N_REP = 8
CAP = 20
TOK = 128
D = 2048
FF = 768
RANK = 32
GROUP = 4
BF = jnp.bfloat16
F32 = jnp.float32
NT = (((1,), (1,)), ((), ()))
NN = (((1,), (0,)), ((), ()))


def dot(a, b, dims=NN):
    return lax.dot_general(a, b, dims, preferred_element_type=F32)


def three(a):
    high = a.astype(BF)
    rest = a - high.astype(F32)
    mid = rest.astype(BF)
    low = (rest - mid.astype(F32)).astype(BF)
    return jnp.concatenate([high, mid, low], axis=0)


def fold(a):
    n = a.shape[0] // 3
    return a[:n] + a[n : 2 * n] + a[2 * n :]


def rows_kernel(z_ref, tokens_ref, meta_ref, rows_ref):
    z = z_ref[0]
    earlier = (
        lax.broadcasted_iota(jnp.int32, (TOK, TOK), 0) < lax.broadcasted_iota(jnp.int32, (TOK, TOK), 1)
    ).astype(F32).astype(BF)
    named, scale = [], []
    for x in range(N_X):
        expert = (x * N_Z + z).astype(F32)
        for b in range(GROUP):
            hit = meta_ref[b, 0:8, :] == expert
            named.append(jnp.sum(jnp.where(hit, 1.0, 0.0), axis=0, keepdims=True))
            scale.append(jnp.sum(jnp.where(hit, meta_ref[b, 8:16, :], 0.0), axis=0, keepdims=True))
    named_all = jnp.concatenate(named, axis=0)
    rank = dot(named_all.astype(BF), earlier)
    slot_of = lax.broadcasted_iota(jnp.int32, (GROUP * CAP, TOK), 0).astype(F32)
    picks, factors = [], []
    for x in range(N_X):
        parts = []
        factor = jnp.zeros((GROUP * CAP, 1), F32)
        for b in range(GROUP):
            i = x * GROUP + b
            target = jnp.where(named[i] > 0.5, rank[i : i + 1, :] + float(b * CAP), -1.0)
            hit = slot_of == target
            parts.append(jnp.where(hit, 1.0, 0.0).astype(BF))
            factor += jnp.sum(jnp.where(hit, scale[i], 0.0), axis=1, keepdims=True)
        picks.append(jnp.concatenate(parts, axis=1))
        factors.append(factor)
    for x in range(N_X):
        for c in range(0, D, 512):
            taken = dot(picks[x], tokens_ref[:, c : c + 512])
            rows_ref[x, :, c : c + 512] = (taken * factors[x]).astype(BF)


def make_rows(z, tokens, meta):
    return pl.pallas_call(
        rows_kernel,
        grid_spec=pltpu.PrefetchScalarGridSpec(
            num_scalar_prefetch=1,
            grid=(N_Z // GROUP,),
            in_specs=[
                pl.BlockSpec((GROUP * TOK, D), lambda g, s: (g, 0)),
                pl.BlockSpec((GROUP, 16, TOK), lambda g, s: (g, 0, 0)),
            ],
            out_specs=pl.BlockSpec((N_X, GROUP * CAP, D), lambda g, s: (0, g, 0)),
        ),
        out_shape=jax.ShapeDtypeStruct((N_X, N_Z * CAP, D), BF),
        compiler_params=pltpu.CompilerParams(vmem_limit_bytes=40 << 20),
        cost_estimate=pl.CostEstimate(flops=3 * 10**9, bytes_accessed=14 << 20, transcendentals=0),
        name="rows",
    )(z, tokens, meta)


def left_kernel(rows_ref, warm_ref, hidden_ref, part_ref):
    projected = fold(dot(three(warm_ref[0]), rows_ref[0], NT))
    part_ref[0] = fold(dot(three(projected), hidden_ref[0]))


def left_part(rows, warm, hidden):
    slots = N_Z * CAP
    return pl.pallas_call(
        left_kernel,
        grid=(N_X,),
        in_specs=[
            pl.BlockSpec((1, slots, D), lambda x: (x, 0, 0)),
            pl.BlockSpec((1, RANK, D), lambda x: (x, 0, 0)),
            pl.BlockSpec((1, slots, FF), lambda x: (x, 0, 0)),
        ],
        out_specs=pl.BlockSpec((1, RANK, FF), lambda x: (x, 0, 0)),
        out_shape=jax.ShapeDtypeStruct((N_X, RANK, FF), F32),
        compiler_params=pltpu.CompilerParams(vmem_limit_bytes=40 << 20),
        cost_estimate=pl.CostEstimate(flops=10**9, bytes_accessed=9 << 20, transcendentals=0),
        name="left",
    )(rows, warm, hidden)


def back_kernel(rows_ref, weight_ref, back_ref, held_ref):
    x = pl.program_id(0)
    for c in range(0, FF, 256):
        held_ref[pl.ds(x, 1), :, c : c + 256] = dot(rows_ref[0], weight_ref[0, c : c + 256, :], NT).astype(BF)[None]

    @pl.when(x == N_X - 1)
    def _():
        span = GROUP * CAP
        n = N_X * span
        to = lax.broadcasted_iota(jnp.int32, (n, n), 0)
        of = lax.broadcasted_iota(jnp.int32, (n, n), 1)
        of_x, of_b, of_c = of // span, (of % span) // CAP, of % CAP
        move = jnp.where(to == of_b * (N_X * CAP) + of_x * CAP + of_c, 1.0, 0.0).astype(BF)
        for g in range(N_Z // GROUP):
            source = jnp.concatenate([held_ref[i, g * span : (g + 1) * span, :] for i in range(N_X)], axis=0)
            moved = dot(move, source).astype(BF)
            for b in range(GROUP):
                back_ref[g * GROUP + b] = moved[b * N_X * CAP : (b + 1) * N_X * CAP]


def back_rows(rows, weights):
    slots = N_Z * CAP
    return pl.pallas_call(
        back_kernel,
        grid=(N_X,),
        in_specs=[
            pl.BlockSpec((1, slots, D), lambda x: (x, 0, 0)),
            pl.BlockSpec((1, FF, D), lambda x: (x, 0, 0)),
        ],
        out_specs=pl.BlockSpec((N_Z, N_X * CAP, FF), lambda x: (0, 0, 0)),
        out_shape=jax.ShapeDtypeStruct((N_Z, N_X * CAP, FF), BF),
        scratch_shapes=[pltpu.VMEM((N_X, slots, FF), BF)],
        compiler_params=pltpu.CompilerParams(vmem_limit_bytes=48 << 20),
        cost_estimate=pl.CostEstimate(flops=5 * 10**9, bytes_accessed=20 << 20, transcendentals=0),
        name="back",
    )(rows, weights)


def right_kernel(basis_ref, hidden_ref, rows_ref, part_ref):
    mapped = fold(dot(three(basis_ref[0]), hidden_ref[0], NT))
    part_ref[0] = fold(dot(three(mapped), rows_ref[0]))


def right_part(basis, hidden, rows):
    slots = N_Z * CAP
    return pl.pallas_call(
        right_kernel,
        grid=(N_X,),
        in_specs=[
            pl.BlockSpec((1, RANK, FF), lambda x: (x, 0, 0)),
            pl.BlockSpec((1, slots, FF), lambda x: (x, 0, 0)),
            pl.BlockSpec((1, slots, D), lambda x: (x, 0, 0)),
        ],
        out_specs=pl.BlockSpec((1, RANK, D), lambda x: (x, 0, 0)),
        out_shape=jax.ShapeDtypeStruct((N_X, RANK, D), F32),
        compiler_params=pltpu.CompilerParams(vmem_limit_bytes=40 << 20),
        cost_estimate=pl.CostEstimate(flops=10**9, bytes_accessed=9 << 20, transcendentals=0),
        name="right",
    )(basis, hidden, rows)


def spread_kernel(place_ref, rows_ref, out_ref):
    count = rows_ref.shape[0]
    pairs = place_ref.shape[0]
    pick = jnp.where(lax.broadcasted_iota(jnp.int32, (pairs, count), 1) == place_ref[...], 1.0, 0.0).astype(BF)
    out_ref[...] = dot(pick, rows_ref[...]).astype(BF).reshape(out_ref.shape)


def spread(place, rows):
    count = rows.shape[0]
    pairs = 256
    return pl.pallas_call(
        spread_kernel,
        grid=(TOK * 8 // pairs,),
        in_specs=[
            pl.BlockSpec((pairs, 1), lambda i: (i, 0)),
            pl.BlockSpec((count, FF), lambda i: (0, 0)),
        ],
        out_specs=pl.BlockSpec((pairs // 8, 8, FF), lambda i: (i, 0, 0)),
        out_shape=jax.ShapeDtypeStruct((TOK, 8, FF), BF),
        compiler_params=pltpu.CompilerParams(vmem_limit_bytes=40 << 20),
        cost_estimate=pl.CostEstimate(flops=2 * 10**9, bytes_accessed=4 << 20, transcendentals=0),
        name="spread",
    )(place, rows)


def gather_tokens(own, z):
    ahead = [(i, (i + 1) % N_Z) for i in range(N_Z)]
    behind = [(i, (i - 1) % N_Z) for i in range(N_Z)]
    tokens = jnp.zeros((N_Z * TOK, D), BF)
    tokens = lax.dynamic_update_slice(tokens, own, (z * TOK, 0))
    right = left = own
    half = TOK // 2
    for step in range(1, N_Z // 2):
        right = lax.ppermute(right, "z", ahead)
        left = lax.ppermute(left, "z", behind)
        tokens = lax.dynamic_update_slice(tokens, right, (lax.rem(z - step + N_Z, N_Z) * TOK, 0))
        tokens = lax.dynamic_update_slice(tokens, left, (lax.rem(z + step, N_Z) * TOK, 0))
    at = lax.rem(z + N_Z // 2, N_Z) * TOK
    tokens = lax.dynamic_update_slice(tokens, lax.ppermute(right[:half], "z", ahead), (at, 0))
    return lax.dynamic_update_slice(tokens, lax.ppermute(left[half:], "z", behind), (at + half, 0))


def places(expert_ids):
    ids = expert_ids
    hit = ids[:, :, None] == jnp.arange(N_X * N_Z, dtype=jnp.int32)[None, None, :]
    named = jnp.any(hit, axis=1)
    earlier = jnp.tril(jnp.ones((TOK, TOK), BF), -1)
    rank = dot(earlier, named.astype(BF))
    slot = jnp.sum(jnp.where(hit, rank[:, None, :], 0.0), axis=2).astype(jnp.int32)
    place = (ids % N_Z) * (N_X * CAP) + (ids // N_Z) * CAP + slot
    return place.reshape(TOK * 8, 1)


def orthonormal(p_sum_t):
    gram = lax.dot_general(
        p_sum_t, p_sum_t, (((2,), (2,)), ((0,), (0,))), precision=lax.Precision.HIGHEST
    )
    factor = jnp.linalg.cholesky(gram)
    return lax.linalg.triangular_solve(factor, p_sum_t, left_side=True, lower=True)


def shards(grad_out, expert_ids, gates, hidden, w_down, q_start):
    x = lax.axis_index("x")
    z = lax.axis_index("z")
    plane = ("x", "y", "c")
    weights = lax.all_gather(w_down[0], plane, axis=0, tiled=True).reshape(N_X, FF, D)
    meta = jnp.concatenate([expert_ids.T.astype(F32), gates.T], axis=0)
    meta = lax.all_gather(meta, "z", axis=0)
    warm = lax.all_gather(q_start[0].T, "x", axis=0)
    stored = lax.all_to_all(hidden.reshape(N_X, N_Z * CAP, FF), "x", split_axis=0, concat_axis=0, tiled=True)
    place = places(expert_ids)
    tokens = gather_tokens(grad_out, z)
    rows = make_rows(z.reshape(1), tokens, meta)
    p_part = left_part(rows, warm, stored)
    back = back_rows(rows, weights)
    returned = lax.all_to_all(back, "z", split_axis=0, concat_axis=0, tiled=True)
    shares = lax.all_to_all(
        p_part.reshape(N_X * N_REP, RANK // N_REP, FF), plane, split_axis=0, concat_axis=0, tiled=True
    )
    p_sum = lax.all_gather(jnp.sum(shares, axis=0), plane, axis=0, tiled=True).reshape(N_X, RANK, FF)
    basis = orthonormal(p_sum)
    q_part = right_part(basis, stored, rows)
    shares = lax.all_to_all(
        q_part.reshape(N_X * N_REP, RANK // N_REP, D), plane, split_axis=0, concat_axis=0, tiled=True
    )
    q_sum = lax.all_gather(jnp.sum(shares, axis=0), ("y", "c"), axis=0, tiled=True)
    p_basis = lax.dynamic_index_in_dim(basis, x, 0, keepdims=False).T * math.sqrt(FF)
    grad_hidden = spread(place, returned.reshape(N_Z * N_X * CAP, FF))
    return (grad_hidden, p_basis[None], (q_sum.T / N_REP)[None])


def solution(mesh):
    fine = Mesh(mesh.devices.reshape(4, 2, N_X, N_Z), ("y", "c", "x", "z"))
    rep, exp = ("y", "c"), ("x", "z")
    in_specs = (
        P(rep + exp, None),
        P(rep + exp, None),
        P(rep + exp, None),
        P(rep, exp, None, None),
        P(exp, rep, None),
        P(exp, None, None),
    )
    out_specs = (P(rep + exp, None, None), P(exp, None, None), P(exp, None, None))
    return jax.shard_map(shards, mesh=fine, in_specs=in_specs, out_specs=out_specs, check_vma=False)
```

```python
import math

import jax
import jax.numpy as jnp
from jax import lax
from jax.experimental import pallas as pl
from jax.experimental.pallas import tpu as pltpu
from jax.sharding import Mesh
from jax.sharding import PartitionSpec as P

N_X = 4
N_Y = 4
N_Z = 16
N_REP = 8
CAP = 20
TOK = 128
D = 2048
FF = 768
RANK = 32
LIMIT = 56 << 20
GROUP = 4
BF = jnp.bfloat16
F32 = jnp.float32
NT = (((1,), (1,)), ((), ()))
NN = (((1,), (0,)), ((), ()))


def dot(a, b, dims=NN):
    return lax.dot_general(a, b, dims, preferred_element_type=F32)


def three(a):
    high = a.astype(BF)
    rest = a - high.astype(F32)
    mid = rest.astype(BF)
    low = (rest - mid.astype(F32)).astype(BF)
    return jnp.concatenate([high, mid, low], axis=0)


def fold(a):
    n = a.shape[0] // 3
    return a[:n] + a[n : 2 * n] + a[2 * n :]


def rows_kernel(z_ref, tokens_ref, meta_ref, warm_ref, hidden_ref, rows_ref, part_ref, warm3_ref):
    z = z_ref[0]

    @pl.when(pl.program_id(0) == 0)
    def _():
        part_ref[...] = jnp.zeros_like(part_ref)
        for x in range(N_X):
            warm3_ref[x] = three(warm_ref[x])

    earlier = (
        lax.broadcasted_iota(jnp.int32, (TOK, TOK), 0) < lax.broadcasted_iota(jnp.int32, (TOK, TOK), 1)
    ).astype(F32).astype(BF)
    named, scale = [], []
    for x in range(N_X):
        expert = (x * N_Z + z).astype(F32)
        for b in range(GROUP):
            hit = meta_ref[b, 0:8, :] == expert
            named.append(jnp.sum(jnp.where(hit, 1.0, 0.0), axis=0, keepdims=True))
            scale.append(jnp.sum(jnp.where(hit, meta_ref[b, 8:16, :], 0.0), axis=0, keepdims=True))
    named_all = jnp.concatenate(named, axis=0)
    rank = dot(named_all.astype(BF), earlier)
    slot_of = lax.broadcasted_iota(jnp.int32, (GROUP * CAP, TOK), 0).astype(F32)
    picks, factors = [], []
    for x in range(N_X):
        parts = []
        factor = jnp.zeros((GROUP * CAP, 1), F32)
        for b in range(GROUP):
            i = x * GROUP + b
            target = jnp.where(named[i] > 0.5, rank[i : i + 1, :] + float(b * CAP), -1.0)
            hit = slot_of == target
            parts.append(jnp.where(hit, 1.0, 0.0).astype(BF))
            factor += jnp.sum(jnp.where(hit, scale[i], 0.0), axis=1, keepdims=True)
        picks.append(jnp.concatenate(parts, axis=1))
        factors.append(factor)
    for x in range(N_X):
        for c in range(0, D, 512):
            taken = dot(picks[x], tokens_ref[:, c : c + 512])
            rows_ref[x, :, c : c + 512] = (taken * factors[x]).astype(BF)
        projected = fold(dot(warm3_ref[x], rows_ref[x], NT))
        part_ref[x] += fold(dot(three(projected), hidden_ref[x]))


def make_rows(z, tokens, meta, warm, hidden):
    return pl.pallas_call(
        rows_kernel,
        grid_spec=pltpu.PrefetchScalarGridSpec(
            num_scalar_prefetch=1,
            grid=(N_Z // GROUP,),
            in_specs=[
                pl.BlockSpec((GROUP * TOK, D), lambda g, s: (g, 0)),
                pl.BlockSpec((GROUP, 16, TOK), lambda g, s: (g, 0, 0)),
                pl.BlockSpec((N_X, RANK, D), lambda g, s: (0, 0, 0)),
                pl.BlockSpec((N_X, GROUP * CAP, FF), lambda g, s: (0, g, 0)),
            ],
            out_specs=[
                pl.BlockSpec((N_X, GROUP * CAP, D), lambda g, s: (0, g, 0)),
                pl.BlockSpec((N_X, RANK, FF), lambda g, s: (0, 0, 0)),
            ],
            scratch_shapes=[pltpu.VMEM((N_X, 3 * RANK, D), BF)],
        ),
        out_shape=[
            jax.ShapeDtypeStruct((N_X, N_Z * CAP, D), BF),
            jax.ShapeDtypeStruct((N_X, RANK, FF), F32),
        ],
        compiler_params=pltpu.CompilerParams(vmem_limit_bytes=LIMIT),
        cost_estimate=pl.CostEstimate(flops=3 * 10**9, bytes_accessed=14 << 20, transcendentals=0),
        name="rows",
    )(z, tokens, meta, warm, hidden)


def back_kernel(rows_ref, weight_ref, back_ref, held_ref):
    x = pl.program_id(0)
    for c in range(0, FF, 256):
        held_ref[pl.ds(x, 1), :, c : c + 256] = dot(rows_ref[0], weight_ref[0, c : c + 256, :], NT).astype(BF)[None]

    @pl.when(x == N_X - 1)
    def _():
        span = GROUP * CAP
        n = N_X * span
        to = lax.broadcasted_iota(jnp.int32, (n, n), 0)
        of = lax.broadcasted_iota(jnp.int32, (n, n), 1)
        of_x, of_b, of_c = of // span, (of % span) // CAP, of % CAP
        move = jnp.where(to == of_b * (N_X * CAP) + of_x * CAP + of_c, 1.0, 0.0).astype(BF)
        for g in range(N_Z // GROUP):
            source = jnp.concatenate([held_ref[i, g * span : (g + 1) * span, :] for i in range(N_X)], axis=0)
            moved = dot(move, source).astype(BF)
            for b in range(GROUP):
                back_ref[g * GROUP + b] = moved[b * N_X * CAP : (b + 1) * N_X * CAP]


def back_rows(rows, weights):
    slots = N_Z * CAP
    return pl.pallas_call(
        back_kernel,
        grid=(N_X,),
        in_specs=[
            pl.BlockSpec((1, slots, D), lambda x: (x, 0, 0)),
            pl.BlockSpec((1, FF, D), lambda x: (x, 0, 0)),
        ],
        out_specs=pl.BlockSpec((N_Z, N_X * CAP, FF), lambda x: (0, 0, 0)),
        out_shape=jax.ShapeDtypeStruct((N_Z, N_X * CAP, FF), BF),
        scratch_shapes=[pltpu.VMEM((N_X, slots, FF), BF)],
        compiler_params=pltpu.CompilerParams(vmem_limit_bytes=LIMIT),
        cost_estimate=pl.CostEstimate(flops=5 * 10**9, bytes_accessed=20 << 20, transcendentals=0),
        name="back",
    )(rows, weights)


def right_kernel(basis_ref, hidden_ref, rows_ref, part_ref):
    mapped = fold(dot(three(basis_ref[0]), hidden_ref[0], NT))
    part_ref[0] = fold(dot(three(mapped), rows_ref[0]))


def right_part(basis, hidden, rows):
    slots = N_Z * CAP
    return pl.pallas_call(
        right_kernel,
        grid=(N_X,),
        in_specs=[
            pl.BlockSpec((1, RANK, FF), lambda x: (x, 0, 0)),
            pl.BlockSpec((1, slots, FF), lambda x: (x, 0, 0)),
            pl.BlockSpec((1, slots, D), lambda x: (x, 0, 0)),
        ],
        out_specs=pl.BlockSpec((1, RANK, D), lambda x: (x, 0, 0)),
        out_shape=jax.ShapeDtypeStruct((N_X, RANK, D), F32),
        compiler_params=pltpu.CompilerParams(vmem_limit_bytes=LIMIT),
        cost_estimate=pl.CostEstimate(flops=10**9, bytes_accessed=9 << 20, transcendentals=0),
        name="right",
    )(basis, hidden, rows)


def spread_kernel(place_ref, rows_ref, out_ref):
    count = rows_ref.shape[0]
    pairs = place_ref.shape[0]
    pick = jnp.where(lax.broadcasted_iota(jnp.int32, (pairs, count), 1) == place_ref[...], 1.0, 0.0).astype(BF)
    out_ref[...] = dot(pick, rows_ref[...]).astype(BF).reshape(out_ref.shape)


def spread(place, rows):
    count = rows.shape[0]
    pairs = 256
    return pl.pallas_call(
        spread_kernel,
        grid=(TOK * 8 // pairs,),
        in_specs=[
            pl.BlockSpec((pairs, 1), lambda i: (i, 0)),
            pl.BlockSpec((count, FF), lambda i: (0, 0)),
        ],
        out_specs=pl.BlockSpec((pairs // 8, 8, FF), lambda i: (i, 0, 0)),
        out_shape=jax.ShapeDtypeStruct((TOK, 8, FF), BF),
        compiler_params=pltpu.CompilerParams(vmem_limit_bytes=LIMIT),
        cost_estimate=pl.CostEstimate(flops=2 * 10**9, bytes_accessed=4 << 20, transcendentals=0),
        name="spread",
    )(place, rows)


def gather_tokens(own, z):
    ahead = [(i, (i + 1) % N_Z) for i in range(N_Z)]
    behind = [(i, (i - 1) % N_Z) for i in range(N_Z)]
    tokens = jnp.zeros((N_Z * TOK, D), BF)
    tokens = lax.dynamic_update_slice(tokens, own, (z * TOK, 0))
    right = left = own
    half = TOK // 2
    for step in range(1, N_Z // 2):
        right = lax.ppermute(right, "z", ahead)
        left = lax.ppermute(left, "z", behind)
        tokens = lax.dynamic_update_slice(tokens, right, (lax.rem(z - step + N_Z, N_Z) * TOK, 0))
        tokens = lax.dynamic_update_slice(tokens, left, (lax.rem(z + step, N_Z) * TOK, 0))
    at = lax.rem(z + N_Z // 2, N_Z) * TOK
    tokens = lax.dynamic_update_slice(tokens, lax.ppermute(right[:half], "z", ahead), (at, 0))
    return lax.dynamic_update_slice(tokens, lax.ppermute(left[half:], "z", behind), (at + half, 0))


def places(expert_ids):
    ids = expert_ids
    hit = ids[:, :, None] == jnp.arange(N_X * N_Z, dtype=jnp.int32)[None, None, :]
    named = jnp.any(hit, axis=1)
    earlier = jnp.tril(jnp.ones((TOK, TOK), BF), -1)
    rank = dot(earlier, named.astype(BF))
    slot = jnp.sum(jnp.where(hit, rank[:, None, :], 0.0), axis=2).astype(jnp.int32)
    place = (ids % N_Z) * (N_X * CAP) + (ids // N_Z) * CAP + slot
    return place.reshape(TOK * 8, 1)


def basis_kernel(sum_ref, basis_ref):
    sums = [sum_ref[x] for x in range(N_X)]
    exact = lax.Precision.HIGHEST
    gram = jnp.stack(
        [lax.dot_general(p, p, NT, precision=exact, preferred_element_type=F32) for p in sums]
    )
    shape = (N_X, RANK, RANK)
    row = lax.broadcasted_iota(jnp.int32, shape, 1)
    column = lax.broadcasted_iota(jnp.int32, shape, 2)
    done = jnp.where(row == column, 1.0, 0.0)
    for j in range(RANK):
        pivot = gram[:, j : j + 1, j : j + 1]
        below = jnp.where(row[:, :, :1] > j, gram[:, :, j : j + 1] / pivot, 0.0)
        scale = jnp.where(row[:, :, :1] == j, lax.rsqrt(pivot), 1.0)
        done = (done - below * done[:, j : j + 1, :]) * scale
        gram = gram - below * gram[:, j : j + 1, :]
    for x in range(N_X):
        basis_ref[x] = lax.dot_general(done[x], sums[x], NN, precision=exact, preferred_element_type=F32)


def orthonormal(p_sum):
    return pl.pallas_call(
        basis_kernel,
        out_shape=jax.ShapeDtypeStruct((N_X, RANK, FF), F32),
        compiler_params=pltpu.CompilerParams(vmem_limit_bytes=LIMIT),
        cost_estimate=pl.CostEstimate(flops=10**7, bytes_accessed=1 << 20, transcendentals=0),
        name="basis",
    )(p_sum)


def sum_right(parts, x):
    total = lax.dynamic_index_in_dim(parts, x, 0, keepdims=False)
    for d in (2, 1, 3):
        piece = lax.dynamic_index_in_dim(parts, lax.rem(x + d, N_X), 0, keepdims=False)
        total = total + lax.ppermute(piece, "x", [(i, (i + d) % N_X) for i in range(N_X)])
    total = total + lax.ppermute(total, "c", [(0, 1), (1, 0)])
    moved = [lax.ppermute(total, "y", [(i, (i + d) % N_Y) for i in range(N_Y)]) for d in (2, 1, 3)]
    return total + moved[0] + (moved[1] + moved[2])


def shards(grad_out, expert_ids, gates, hidden, w_down, q_start):
    x = lax.axis_index("x")
    z = lax.axis_index("z")
    plane = ("x", "y", "c")
    weights = lax.all_gather(w_down[0], plane, axis=0, tiled=True).reshape(N_X, FF, D)
    meta = jnp.concatenate([expert_ids.T.astype(F32), gates.T], axis=0)
    meta = lax.all_to_all(
        jnp.broadcast_to(meta[None], (N_Z,) + meta.shape), "z", split_axis=0, concat_axis=0, tiled=True
    )
    warm = lax.all_gather(q_start[0].T, "x", axis=0)
    stored = lax.all_to_all(hidden.reshape(N_X, N_Z * CAP, FF), "x", split_axis=0, concat_axis=0, tiled=True)
    place = places(expert_ids)
    tokens = gather_tokens(grad_out, z)
    rows, p_part = make_rows(z.reshape(1), tokens, meta, warm, stored)
    back = back_rows(rows, weights)
    returned = lax.all_to_all(back, "z", split_axis=0, concat_axis=0, tiled=True)
    shares = lax.all_to_all(
        p_part.reshape(N_X * N_REP, RANK // N_REP, FF), plane, split_axis=0, concat_axis=0, tiled=True
    )
    p_sum = lax.all_gather(jnp.sum(shares, axis=0), plane, axis=0, tiled=True).reshape(N_X, RANK, FF)
    basis = orthonormal(p_sum)
    q_sum = sum_right(right_part(basis, stored, rows), x)
    p_basis = lax.dynamic_index_in_dim(basis, x, 0, keepdims=False).T * math.sqrt(FF)
    grad_hidden = spread(place, returned.reshape(N_Z * N_X * CAP, FF))
    return (grad_hidden, p_basis[None], (q_sum.T / N_REP)[None])


def solution(mesh):
    fine = Mesh(mesh.devices.reshape(N_Y, 2, N_X, N_Z), ("y", "c", "x", "z"))
    rep, exp = ("y", "c"), ("x", "z")
    in_specs = (
        P(rep + exp, None),
        P(rep + exp, None),
        P(rep + exp, None),
        P(rep, exp, None, None),
        P(exp, rep, None),
        P(exp, None, None),
    )
    out_specs = (P(rep + exp, None, None), P(exp, None, None), P(exp, None, None))
    return jax.shard_map(shards, mesh=fine, in_specs=in_specs, out_specs=out_specs, check_vma=False)
```

```python
import math

import jax
import jax.numpy as jnp
from jax import lax
from jax.experimental import pallas as pl
from jax.experimental.pallas import tpu as pltpu
from jax.sharding import Mesh
from jax.sharding import PartitionSpec as P

N_X = 4
N_Y = 4
N_Z = 16
N_REP = 8
CAP = 20
TOK = 128
D = 2048
FF = 768
RANK = 32
LIMIT = 56 << 20
GROUP = 4
GROUPS = N_Z // GROUP
SPAN = GROUP * CAP
SLOTS = N_Z * CAP
SHARE = FF // N_REP
PAD = 16
OFFSETS = [-((j + 1) // 2) if j % 2 else j // 2 for j in range(N_Z)]
BF = jnp.bfloat16
F32 = jnp.float32
NT = (((1,), (1,)), ((), ()))
NN = (((1,), (0,)), ((), ()))


def dot(a, b, dims=NN):
    return lax.dot_general(a, b, dims, preferred_element_type=F32)


def three(a):
    high = a.astype(BF)
    rest = a - high.astype(F32)
    mid = rest.astype(BF)
    low = (rest - mid.astype(F32)).astype(BF)
    return jnp.concatenate([high, mid, low], axis=0)


def fold(a):
    n = a.shape[0] // 3
    return a[:n] + a[n : 2 * n] + a[2 * n :]


def offset(j):
    return jnp.where(j % 2 == 1, -((j + 1) // 2), j // 2)


def picks_kernel(z_ref, meta_ref, picks_ref, scale_ref, order_ref, move_ref):
    z = z_ref[0]
    earlier = (
        lax.broadcasted_iota(jnp.int32, (TOK, TOK), 0) < lax.broadcasted_iota(jnp.int32, (TOK, TOK), 1)
    ).astype(F32).astype(BF)
    slot_of = lax.broadcasted_iota(jnp.int32, (SPAN, TOK), 0).astype(F32)
    for g in range(GROUPS):
        named, gate = [], []
        for x in range(N_X):
            expert = (x * N_Z + z).astype(F32)
            for b in range(GROUP):
                at = lax.rem(z + OFFSETS[g * GROUP + b] + N_Z, N_Z)
                hit = meta_ref[at, 0:8, :] == expert
                named.append(jnp.sum(jnp.where(hit, 1.0, 0.0), axis=0, keepdims=True))
                gate.append(jnp.sum(jnp.where(hit, meta_ref[at, 8:16, :], 0.0), axis=0, keepdims=True))
        rank = dot(jnp.concatenate(named, axis=0).astype(BF), earlier)
        for x in range(N_X):
            scale = jnp.zeros((SPAN, 1), F32)
            for b in range(GROUP):
                i = x * GROUP + b
                target = jnp.where(named[i] > 0.5, rank[i : i + 1, :] + float(b * CAP), -1.0)
                hit = slot_of == target
                picks_ref[g, x * SPAN : (x + 1) * SPAN, b * TOK : (b + 1) * TOK] = jnp.where(hit, 1.0, 0.0).astype(BF)
                scale += jnp.sum(jnp.where(hit, gate[i], 0.0), axis=1, keepdims=True)
            scale_ref[g, x * SPAN : (x + 1) * SPAN, :] = jnp.broadcast_to(scale, (SPAN, 128))
    came = lax.broadcasted_iota(jnp.int32, (SLOTS, SLOTS), 0)
    own = lax.broadcasted_iota(jnp.int32, (SLOTS, SLOTS), 1)
    block = lax.rem(z + offset(came // CAP) + N_Z, N_Z)
    order_ref[...] = jnp.where(own == block * CAP + came % CAP, 1.0, 0.0).astype(BF)
    x, b, k = own // SPAN, (own % SPAN) // CAP, own % CAP
    move_ref[...] = jnp.where(came == b * (N_X * CAP) + x * CAP + k, 1.0, 0.0).astype(BF)


def make_picks(z, meta):
    slots = N_X * SPAN
    return pl.pallas_call(
        picks_kernel,
        in_specs=[pl.BlockSpec(memory_space=pltpu.SMEM), pl.BlockSpec(memory_space=pltpu.VMEM)],
        out_specs=[pl.BlockSpec(memory_space=pltpu.VMEM)] * 4,
        out_shape=[
            jax.ShapeDtypeStruct((GROUPS, slots, GROUP * TOK), BF),
            jax.ShapeDtypeStruct((GROUPS, slots, 128), F32),
            jax.ShapeDtypeStruct((SLOTS, SLOTS), BF),
            jax.ShapeDtypeStruct((SLOTS, SLOTS), BF),
        ],
        compiler_params=pltpu.CompilerParams(vmem_limit_bytes=LIMIT),
        cost_estimate=pl.CostEstimate(flops=10**7, bytes_accessed=4 << 20, transcendentals=0),
        name="picks",
    )(z, meta)


def rows_kernel(picks_ref, scale_ref, *refs):
    rows_ref = refs[-1]
    tokens = jnp.concatenate([ref[...] for ref in refs[:-1]], axis=0)
    for c in range(0, tokens.shape[1], 512):
        taken = dot(picks_ref[0], tokens[:, c : c + 512])
        for x in range(N_X):
            scale = scale_ref[0, x * SPAN : (x + 1) * SPAN, :1]
            rows_ref[x, :, c : c + 512] = (taken[x * SPAN : (x + 1) * SPAN] * scale).astype(BF)


def make_rows(group, picks, scale, blocks):
    slots = N_X * SPAN
    wide = D // 2
    return pl.pallas_call(
        rows_kernel,
        grid=(D // wide,),
        in_specs=[
            pl.BlockSpec((1, slots, GROUP * TOK), lambda i: (group, 0, 0)),
            pl.BlockSpec((1, slots, 128), lambda i: (group, 0, 0)),
        ]
        + [pl.BlockSpec((block.shape[0], wide), lambda i: (0, i)) for block in blocks],
        out_specs=pl.BlockSpec((N_X, SPAN, wide), lambda i: (0, 0, i)),
        out_shape=jax.ShapeDtypeStruct((N_X, SPAN, D), BF),
        compiler_params=pltpu.CompilerParams(vmem_limit_bytes=LIMIT),
        cost_estimate=pl.CostEstimate(flops=7 * 10**8, bytes_accessed=4 << 20, transcendentals=0),
        name="rows",
    )(picks, scale, *blocks)


def all_rows(refs):
    return jnp.concatenate([ref[0] for ref in refs], axis=0)


def unfold(a):
    a = a.reshape(N_REP, PAD, a.shape[1])
    k = RANK // N_REP
    return (a[:, :k] + a[:, k : 2 * k] + a[:, 2 * k : 3 * k]).reshape(RANK, a.shape[2])


def project_kernel(gathered_ref, order_ref, *refs):
    projected = unfold(dot(gathered_ref[0].reshape(N_REP * PAD, D), all_rows(refs[:-1]), NT))
    refs[-1][0] = dot(three(projected), order_ref[...]).astype(BF)


def project(gathered, order, rows):
    slots = len(rows) * SPAN
    return pl.pallas_call(
        project_kernel,
        grid=(N_X,),
        in_specs=[
            pl.BlockSpec((1, N_REP, PAD, D), lambda x: (x, 0, SHARE // PAD, 0)),
            pl.BlockSpec((slots, SLOTS), lambda x: (0, 0)),
        ]
        + [pl.BlockSpec((1, SPAN, D), lambda x: (x, 0, 0))] * len(rows),
        out_specs=pl.BlockSpec((1, 3 * RANK, SLOTS), lambda x: (x, 0, 0)),
        out_shape=jax.ShapeDtypeStruct((N_X, 3 * RANK, SLOTS), BF),
        compiler_params=pltpu.CompilerParams(vmem_limit_bytes=LIMIT),
        cost_estimate=pl.CostEstimate(flops=10**9, bytes_accessed=6 << 20, transcendentals=0),
        name="project",
    )(gathered, order, *rows)


def left_kernel(near_ref, gathered_ref, rows_ref, hidden_ref, order_ref, part_ref):
    projected = unfold(dot(gathered_ref[0].reshape(N_REP * PAD, D), rows_ref[0], NT))
    ordered = near_ref[0] + dot(three(projected), order_ref[...]).astype(BF)
    part_ref[...] = fold(dot(ordered, hidden_ref[0])).reshape(part_ref.shape)


def left_part(near, gathered, rows, hidden, order):
    last = GROUPS - 1
    return pl.pallas_call(
        left_kernel,
        grid=(N_X,),
        in_specs=[
            pl.BlockSpec((1, 3 * RANK, SLOTS), lambda x: (x, 0, 0)),
            pl.BlockSpec((1, N_REP, PAD, D), lambda x: (x, 0, SHARE // PAD, 0)),
            pl.BlockSpec((1, SPAN, D), lambda x: (x, 0, 0)),
            pl.BlockSpec((1, SLOTS, FF), lambda x: (x, 0, 0)),
            pl.BlockSpec((SPAN, SLOTS), lambda x: (last, 0)),
        ],
        out_specs=pl.BlockSpec((N_REP, RANK // N_REP, FF), lambda x: (x, 0, 0)),
        out_shape=jax.ShapeDtypeStruct((N_X * N_REP, RANK // N_REP, FF), F32),
        compiler_params=pltpu.CompilerParams(vmem_limit_bytes=LIMIT),
        cost_estimate=pl.CostEstimate(flops=10**9, bytes_accessed=6 << 20, transcendentals=0),
        name="left",
    )(near, gathered, rows, hidden, order)


def back_kernel(z_ref, gathered_ref, move_ref, *refs):
    back_ref, held_ref = refs[-2:]
    x = pl.program_id(0)
    z = z_ref[0]
    weight = gathered_ref[0, :, :SHARE, :].reshape(FF, D)
    rows = all_rows(refs[:-2])
    for c in range(0, FF, 256):
        held_ref[pl.ds(x, 1), :, c : c + 256] = dot(rows, weight[c : c + 256], NT).astype(BF)[None]

    @pl.when(x == N_X - 1)
    def _():
        for g in range(GROUPS):
            source = jnp.concatenate([held_ref[i, g * SPAN : (g + 1) * SPAN, :] for i in range(N_X)], axis=0)
            moved = dot(move_ref[...], source).astype(BF)
            for b in range(GROUP):
                at = lax.rem(z + OFFSETS[g * GROUP + b] + N_Z, N_Z)
                back_ref[pl.ds(at, 1)] = moved[b * N_X * CAP : (b + 1) * N_X * CAP][None]


def back_rows(z, gathered, move, rows):
    return pl.pallas_call(
        back_kernel,
        grid_spec=pltpu.PrefetchScalarGridSpec(
            num_scalar_prefetch=1,
            grid=(N_X,),
            in_specs=[
                pl.BlockSpec((1, N_REP, SHARE + PAD, D), lambda x, s: (x, 0, 0, 0)),
                pl.BlockSpec((SLOTS, SLOTS), lambda x, s: (0, 0)),
            ]
            + [pl.BlockSpec((1, SPAN, D), lambda x, s: (x, 0, 0))] * GROUPS,
            out_specs=pl.BlockSpec((N_Z, N_X * CAP, FF), lambda x, s: (0, 0, 0)),
            scratch_shapes=[pltpu.VMEM((N_X, SLOTS, FF), BF)],
        ),
        out_shape=jax.ShapeDtypeStruct((N_Z, N_X * CAP, FF), BF),
        compiler_params=pltpu.CompilerParams(vmem_limit_bytes=LIMIT),
        cost_estimate=pl.CostEstimate(flops=4 * 10**9, bytes_accessed=20 << 20, transcendentals=0),
        name="back",
    )(z, gathered, move, *rows)


def right_kernel(basis_ref, hidden_ref, order_ref, *refs):
    part_ref = refs[-1]
    mapped = fold(dot(three(basis_ref[0]), hidden_ref[0], NT))
    ordered = dot(three(mapped), order_ref[...], NT).astype(BF)
    part_ref[0] = fold(dot(ordered, all_rows(refs[:-1])))


def right_part(basis, hidden, order, rows):
    return pl.pallas_call(
        right_kernel,
        grid=(N_X,),
        in_specs=[
            pl.BlockSpec((1, RANK, FF), lambda x: (x, 0, 0)),
            pl.BlockSpec((1, SLOTS, FF), lambda x: (x, 0, 0)),
            pl.BlockSpec((SLOTS, SLOTS), lambda x: (0, 0)),
        ]
        + [pl.BlockSpec((1, SPAN, D), lambda x: (x, 0, 0))] * GROUPS,
        out_specs=pl.BlockSpec((1, RANK, D), lambda x: (x, 0, 0)),
        out_shape=jax.ShapeDtypeStruct((N_X, RANK, D), F32),
        compiler_params=pltpu.CompilerParams(vmem_limit_bytes=LIMIT),
        cost_estimate=pl.CostEstimate(flops=10**9, bytes_accessed=9 << 20, transcendentals=0),
        name="right",
    )(basis, hidden, order, *rows)


def spread_kernel(place_ref, rows_ref, out_ref):
    count = rows_ref.shape[0]
    pairs = place_ref.shape[0]
    pick = jnp.where(lax.broadcasted_iota(jnp.int32, (pairs, count), 1) == place_ref[...], 1.0, 0.0).astype(BF)
    out_ref[...] = dot(pick, rows_ref[...]).astype(BF).reshape(out_ref.shape)


def spread(place, rows):
    count = rows.shape[0]
    pairs = 256
    return pl.pallas_call(
        spread_kernel,
        grid=(TOK * 8 // pairs,),
        in_specs=[
            pl.BlockSpec((pairs, 1), lambda i: (i, 0)),
            pl.BlockSpec((count, FF), lambda i: (0, 0)),
        ],
        out_specs=pl.BlockSpec((pairs // 8, 8, FF), lambda i: (i, 0, 0)),
        out_shape=jax.ShapeDtypeStruct((TOK, 8, FF), BF),
        compiler_params=pltpu.CompilerParams(vmem_limit_bytes=LIMIT),
        cost_estimate=pl.CostEstimate(flops=2 * 10**9, bytes_accessed=4 << 20, transcendentals=0),
        name="spread",
    )(place, rows)


def turn(n, d):
    return [(i, (i + d) % n) for i in range(n)]


def places(expert_ids):
    ids = expert_ids
    hit = ids[:, :, None] == jnp.arange(N_X * N_Z, dtype=jnp.int32)[None, None, :]
    named = jnp.any(hit, axis=1)
    earlier = jnp.tril(jnp.ones((TOK, TOK), BF), -1)
    rank = dot(earlier, named.astype(BF))
    slot = jnp.sum(jnp.where(hit, rank[:, None, :], 0.0), axis=2).astype(jnp.int32)
    place = (ids % N_Z) * (N_X * CAP) + (ids // N_Z) * CAP + slot
    return place.reshape(TOK * 8, 1)


def basis_kernel(sum_ref, basis_ref):
    sums = [sum_ref[x * RANK : (x + 1) * RANK, :] for x in range(N_X)]
    exact = lax.Precision.HIGHEST
    gram = jnp.stack(
        [lax.dot_general(p, p, NT, precision=exact, preferred_element_type=F32) for p in sums]
    )
    shape = (N_X, RANK, RANK)
    row = lax.broadcasted_iota(jnp.int32, shape, 1)
    column = lax.broadcasted_iota(jnp.int32, shape, 2)
    done = jnp.where(row == column, 1.0, 0.0)
    for j in range(RANK):
        pivot = gram[:, j : j + 1, j : j + 1]
        below = jnp.where(row[:, :, :1] > j, gram[:, :, j : j + 1] / pivot, 0.0)
        scale = jnp.where(row[:, :, :1] == j, lax.rsqrt(pivot), 1.0)
        done = (done - below * done[:, j : j + 1, :]) * scale
        gram = gram - below * gram[:, j : j + 1, :]
    for x in range(N_X):
        basis_ref[x] = lax.dot_general(done[x], sums[x], NN, precision=exact, preferred_element_type=F32)


def orthonormal(p_sum):
    return pl.pallas_call(
        basis_kernel,
        out_shape=jax.ShapeDtypeStruct((N_X, RANK, FF), F32),
        compiler_params=pltpu.CompilerParams(vmem_limit_bytes=LIMIT),
        cost_estimate=pl.CostEstimate(flops=10**7, bytes_accessed=1 << 20, transcendentals=0),
        name="basis",
    )(p_sum)


def sum_right(parts, x):
    total = lax.dynamic_index_in_dim(parts, x, 0, keepdims=False)
    for d in (2, 1, 3):
        piece = lax.dynamic_index_in_dim(parts, lax.rem(x + d, N_X), 0, keepdims=False)
        total = total + lax.ppermute(piece, "x", turn(N_X, d))
    total = total + lax.ppermute(total, "c", turn(2, 1))
    moved = [lax.ppermute(total, "y", turn(N_Y, d)) for d in (2, 1, 3)]
    return total + moved[0] + (moved[1] + moved[2])


def shards(grad_out, expert_ids, gates, hidden, w_down, q_start):
    x, z = lax.axis_index("x"), lax.axis_index("z")
    plane = ("x", "y", "c")
    at = z.reshape(1)
    k = RANK // N_REP
    rep = lax.axis_index("y") * 2 + lax.axis_index("c")
    warm = three(lax.dynamic_slice(q_start[0].T, (rep * k, 0), (k, D)))
    warm = jnp.pad(warm, ((0, PAD - 3 * k), (0, 0)))
    gathered = lax.all_gather(jnp.concatenate([w_down[0], warm], axis=0), plane, axis=0, tiled=True)
    gathered = gathered.reshape(N_X, N_REP, SHARE + PAD, D)
    meta = jnp.concatenate([expert_ids.T.astype(F32), gates.T], axis=0)
    meta = lax.all_to_all(
        jnp.broadcast_to(meta[None], (N_Z,) + meta.shape), "z", split_axis=0, concat_axis=0, tiled=True
    )
    stored = lax.all_to_all(hidden.reshape(N_X, SLOTS, FF), "x", split_axis=0, concat_axis=0, tiled=True)

    blocks = [grad_out]
    right = left = grad_out
    rows = []
    for step in range(1, N_Z // 2):
        before = (right, left)
        right = lax.ppermute(right, "z", turn(N_Z, 1))
        left = lax.ppermute(left, "z", turn(N_Z, -1))
        beside = []
        if step == 1:
            beside = [meta]
        elif step == 2:
            picks, scale, order, move = make_picks(at, meta)
            beside = [picks]
        elif step == 3 or step == 5 or step == 7:
            g = len(rows)
            rows.append(make_rows(g, picks, scale, blocks[g * GROUP : (g + 1) * GROUP]))
            beside = [rows[g]]
        now = (right, left)
        right, _, *beside = lax.optimization_barrier((right, before[1], *beside))
        left, _ = lax.optimization_barrier((left, before[0]))
        if step == 1:
            meta = beside[0]
        blocks += [*now]
    half = TOK // 2
    last = blocks[12:] + [
        lax.ppermute(right[:half], "z", turn(N_Z, 1)),
        lax.ppermute(left[half:], "z", turn(N_Z, -1)),
    ]
    near = project(gathered, order, rows)
    last, near = lax.optimization_barrier((last, near))
    rows.append(make_rows(3, picks, scale, last))
    p_part = left_part(near, gathered, rows[-1], stored, order)
    back = back_rows(at, gathered, move, rows)
    returned = lax.all_to_all(back, "z", split_axis=0, concat_axis=0, tiled=True)
    shares = lax.all_to_all(p_part, plane, split_axis=0, concat_axis=0, tiled=True)
    basis = orthonormal(lax.all_gather(jnp.sum(shares, axis=0), plane, axis=0, tiled=True))
    q_sum = sum_right(right_part(basis, stored, order, rows), x)
    p_basis = lax.dynamic_index_in_dim(basis, x, 0, keepdims=False).T * math.sqrt(FF)
    place = places(expert_ids)
    grad_hidden = spread(place, returned.reshape(N_Z * N_X * CAP, FF))
    return (grad_hidden, p_basis[None], (q_sum.T / N_REP)[None])


def solution(mesh):
    fine = Mesh(mesh.devices.reshape(N_Y, 2, N_X, N_Z), ("y", "c", "x", "z"))
    rep, exp = ("y", "c"), ("x", "z")
    in_specs = (
        P(rep + exp, None),
        P(rep + exp, None),
        P(rep + exp, None),
        P(rep, exp, None, None),
        P(exp, rep, None),
        P(exp, None, None),
    )
    out_specs = (P(rep + exp, None, None), P(exp, None, None), P(exp, None, None))
    return jax.shard_map(shards, mesh=fine, in_specs=in_specs, out_specs=out_specs, check_vma=False)
```

```python
import math

import jax
import jax.numpy as jnp
from jax import lax
from jax.experimental import pallas as pl
from jax.experimental.pallas import tpu as pltpu
from jax.sharding import Mesh
from jax.sharding import PartitionSpec as P

N_X = 4
N_Y = 4
N_Z = 16
N_REP = 8
CAP = 20
TOK = 128
D = 2048
FF = 768
RANK = 32
LIMIT = 56 << 20
GROUP = 4
GROUPS = N_Z // GROUP
SPAN = GROUP * CAP
SLOTS = N_Z * CAP
SHARE = FF // N_REP
PAD = 16
OFFSETS = [-((j + 1) // 2) if j % 2 else j // 2 for j in range(N_Z)]
BF = jnp.bfloat16
F32 = jnp.float32
NT = (((1,), (1,)), ((), ()))
NN = (((1,), (0,)), ((), ()))


def dot(a, b, dims=NN):
    return lax.dot_general(a, b, dims, preferred_element_type=F32)


def three(a):
    high = a.astype(BF)
    rest = a - high.astype(F32)
    mid = rest.astype(BF)
    low = (rest - mid.astype(F32)).astype(BF)
    return jnp.concatenate([high, mid, low], axis=0)


def three_outside(a):
    high = lax.reduce_precision(a, 8, 7)
    mid = lax.reduce_precision(a - high, 8, 7)
    return jnp.concatenate([high, mid, a - high - mid], axis=0).astype(BF)


def fold(a):
    n = a.shape[0] // 3
    return a[:n] + a[n : 2 * n] + a[2 * n :]


def offset(j):
    return jnp.where(j % 2 == 1, -((j + 1) // 2), j // 2)


def picks_kernel(z_ref, meta_ref, picks_ref, scale_ref, order_ref, move_ref):
    z = z_ref[0]
    earlier = (
        lax.broadcasted_iota(jnp.int32, (TOK, TOK), 0) < lax.broadcasted_iota(jnp.int32, (TOK, TOK), 1)
    ).astype(F32).astype(BF)
    slot_of = lax.broadcasted_iota(jnp.int32, (SPAN, TOK), 0).astype(F32)
    for g in range(GROUPS):
        named, gate = [], []
        for x in range(N_X):
            expert = (x * N_Z + z).astype(F32)
            for b in range(GROUP):
                at = lax.rem(z + OFFSETS[g * GROUP + b] + N_Z, N_Z)
                hit = meta_ref[at, 0:8, :] == expert
                named.append(jnp.sum(jnp.where(hit, 1.0, 0.0), axis=0, keepdims=True))
                gate.append(jnp.sum(jnp.where(hit, meta_ref[at, 8:16, :], 0.0), axis=0, keepdims=True))
        rank = dot(jnp.concatenate(named, axis=0).astype(BF), earlier)
        for x in range(N_X):
            scale = jnp.zeros((SPAN, 1), F32)
            for b in range(GROUP):
                i = x * GROUP + b
                target = jnp.where(named[i] > 0.5, rank[i : i + 1, :] + float(b * CAP), -1.0)
                hit = slot_of == target
                picks_ref[g, x * SPAN : (x + 1) * SPAN, b * TOK : (b + 1) * TOK] = jnp.where(hit, 1.0, 0.0).astype(BF)
                scale += jnp.sum(jnp.where(hit, gate[i], 0.0), axis=1, keepdims=True)
            scale_ref[g, x * SPAN : (x + 1) * SPAN, :] = jnp.broadcast_to(scale, (SPAN, 128))
    came = lax.broadcasted_iota(jnp.int32, (SLOTS, SLOTS), 0)
    own = lax.broadcasted_iota(jnp.int32, (SLOTS, SLOTS), 1)
    block = lax.rem(z + offset(came // CAP) + N_Z, N_Z)
    order_ref[...] = jnp.where(own == block * CAP + came % CAP, 1.0, 0.0).astype(BF)
    x, b, k = own // SPAN, (own % SPAN) // CAP, own % CAP
    move_ref[...] = jnp.where(came == b * (N_X * CAP) + x * CAP + k, 1.0, 0.0).astype(BF)


def make_picks(z, meta):
    slots = N_X * SPAN
    return pl.pallas_call(
        picks_kernel,
        in_specs=[pl.BlockSpec(memory_space=pltpu.SMEM), pl.BlockSpec(memory_space=pltpu.VMEM)],
        out_specs=[pl.BlockSpec(memory_space=pltpu.VMEM)] * 4,
        out_shape=[
            jax.ShapeDtypeStruct((GROUPS, slots, GROUP * TOK), BF),
            jax.ShapeDtypeStruct((GROUPS, slots, 128), F32),
            jax.ShapeDtypeStruct((SLOTS, SLOTS), BF),
            jax.ShapeDtypeStruct((SLOTS, SLOTS), BF),
        ],
        compiler_params=pltpu.CompilerParams(vmem_limit_bytes=LIMIT),
        cost_estimate=pl.CostEstimate(flops=10**7, bytes_accessed=4 << 20, transcendentals=0),
        name="picks",
    )(z, meta)


def rows_kernel(picks_ref, scale_ref, *refs):
    rows_ref = refs[-1]
    tokens = jnp.concatenate([ref[...] for ref in refs[:-1]], axis=0)
    for c in range(0, tokens.shape[1], 512):
        taken = dot(picks_ref[0], tokens[:, c : c + 512])
        for x in range(N_X):
            scale = scale_ref[0, x * SPAN : (x + 1) * SPAN, :1]
            rows_ref[x, :, c : c + 512] = (taken[x * SPAN : (x + 1) * SPAN] * scale).astype(BF)


def make_rows(group, picks, scale, blocks):
    slots = N_X * SPAN
    wide = D // 2
    return pl.pallas_call(
        rows_kernel,
        grid=(D // wide,),
        in_specs=[
            pl.BlockSpec((1, slots, GROUP * TOK), lambda i: (group, 0, 0)),
            pl.BlockSpec((1, slots, 128), lambda i: (group, 0, 0)),
        ]
        + [pl.BlockSpec((block.shape[0], wide), lambda i: (0, i)) for block in blocks],
        out_specs=pl.BlockSpec((N_X, SPAN, wide), lambda i: (0, 0, i)),
        out_shape=jax.ShapeDtypeStruct((N_X, SPAN, D), BF),
        compiler_params=pltpu.CompilerParams(vmem_limit_bytes=LIMIT),
        cost_estimate=pl.CostEstimate(flops=7 * 10**8, bytes_accessed=4 << 20, transcendentals=0),
        name="rows",
    )(picks, scale, *blocks)


def all_rows(refs):
    return jnp.concatenate([ref[0] for ref in refs], axis=0)


def unfold(a):
    a = a.reshape(N_REP, PAD, a.shape[1])
    k = RANK // N_REP
    return (a[:, :k] + a[:, k : 2 * k] + a[:, 2 * k : 3 * k]).reshape(RANK, a.shape[2])


def project_kernel(gathered_ref, order_ref, *refs):
    projected = unfold(dot(gathered_ref[0].reshape(N_REP * PAD, D), all_rows(refs[:-1]), NT))
    refs[-1][0] = dot(three(projected), order_ref[...]).astype(BF)


def project(gathered, order, rows):
    slots = len(rows) * SPAN
    return pl.pallas_call(
        project_kernel,
        grid=(N_X,),
        in_specs=[
            pl.BlockSpec((1, N_REP, PAD, D), lambda x: (x, 0, SHARE // PAD, 0)),
            pl.BlockSpec((slots, SLOTS), lambda x: (0, 0)),
        ]
        + [pl.BlockSpec((1, SPAN, D), lambda x: (x, 0, 0))] * len(rows),
        out_specs=pl.BlockSpec((1, 3 * RANK, SLOTS), lambda x: (x, 0, 0)),
        out_shape=jax.ShapeDtypeStruct((N_X, 3 * RANK, SLOTS), BF),
        compiler_params=pltpu.CompilerParams(vmem_limit_bytes=LIMIT),
        cost_estimate=pl.CostEstimate(flops=10**9, bytes_accessed=6 << 20, transcendentals=0),
        name="project",
    )(gathered, order, *rows)


def left_kernel(near_ref, gathered_ref, rows_ref, hidden_ref, order_ref, part_ref):
    projected = unfold(dot(gathered_ref[0].reshape(N_REP * PAD, D), rows_ref[0], NT))
    ordered = near_ref[0] + dot(three(projected), order_ref[...]).astype(BF)
    part_ref[0] = fold(dot(ordered, hidden_ref[0]))


def left_part(near, gathered, rows, hidden, order):
    last = GROUPS - 1
    return pl.pallas_call(
        left_kernel,
        grid=(N_X,),
        in_specs=[
            pl.BlockSpec((1, 3 * RANK, SLOTS), lambda x: (x, 0, 0)),
            pl.BlockSpec((1, N_REP, PAD, D), lambda x: (x, 0, SHARE // PAD, 0)),
            pl.BlockSpec((1, SPAN, D), lambda x: (x, 0, 0)),
            pl.BlockSpec((1, SLOTS, FF), lambda x: (x, 0, 0)),
            pl.BlockSpec((SPAN, SLOTS), lambda x: (last, 0)),
        ],
        out_specs=pl.BlockSpec((1, RANK, FF), lambda x: (x, 0, 0)),
        out_shape=jax.ShapeDtypeStruct((N_X, RANK, FF), F32),
        compiler_params=pltpu.CompilerParams(vmem_limit_bytes=LIMIT),
        cost_estimate=pl.CostEstimate(flops=10**9, bytes_accessed=6 << 20, transcendentals=0),
        name="left",
    )(near, gathered, rows, hidden, order)


def back_kernel(z_ref, gathered_ref, move_ref, *refs):
    back_ref, held_ref = refs[-2:]
    x = pl.program_id(0)
    z = z_ref[0]
    weight = gathered_ref[0, :, :SHARE, :].reshape(FF, D)
    rows = all_rows(refs[:-2])
    for c in range(0, FF, 256):
        held_ref[pl.ds(x, 1), :, c : c + 256] = dot(rows, weight[c : c + 256], NT).astype(BF)[None]

    @pl.when(x == N_X - 1)
    def _():
        for g in range(GROUPS):
            source = jnp.concatenate([held_ref[i, g * SPAN : (g + 1) * SPAN, :] for i in range(N_X)], axis=0)
            moved = dot(move_ref[...], source).astype(BF)
            for b in range(GROUP):
                at = lax.rem(z + OFFSETS[g * GROUP + b] + N_Z, N_Z)
                back_ref[pl.ds(at, 1)] = moved[b * N_X * CAP : (b + 1) * N_X * CAP][None]


def back_rows(z, gathered, move, rows):
    return pl.pallas_call(
        back_kernel,
        grid_spec=pltpu.PrefetchScalarGridSpec(
            num_scalar_prefetch=1,
            grid=(N_X,),
            in_specs=[
                pl.BlockSpec((1, N_REP, SHARE + PAD, D), lambda x, s: (x, 0, 0, 0)),
                pl.BlockSpec((SLOTS, SLOTS), lambda x, s: (0, 0)),
            ]
            + [pl.BlockSpec((1, SPAN, D), lambda x, s: (x, 0, 0))] * GROUPS,
            out_specs=pl.BlockSpec((N_Z, N_X * CAP, FF), lambda x, s: (0, 0, 0)),
            scratch_shapes=[pltpu.VMEM((N_X, SLOTS, FF), BF)],
        ),
        out_shape=jax.ShapeDtypeStruct((N_Z, N_X * CAP, FF), BF),
        compiler_params=pltpu.CompilerParams(vmem_limit_bytes=LIMIT),
        cost_estimate=pl.CostEstimate(flops=4 * 10**9, bytes_accessed=20 << 20, transcendentals=0),
        name="back",
    )(z, gathered, move, *rows)


def right_kernel(basis_ref, hidden_ref, order_ref, *refs):
    part_ref = refs[-1]
    mapped = fold(dot(three(basis_ref[0]), hidden_ref[0], NT))
    ordered = dot(three(mapped), order_ref[...], NT).astype(BF)
    part_ref[0] = fold(dot(ordered, all_rows(refs[:-1])))


def right_part(basis, hidden, order, rows):
    return pl.pallas_call(
        right_kernel,
        grid=(N_X,),
        in_specs=[
            pl.BlockSpec((1, RANK, FF), lambda x: (x, 0, 0)),
            pl.BlockSpec((1, SLOTS, FF), lambda x: (x, 0, 0)),
            pl.BlockSpec((SLOTS, SLOTS), lambda x: (0, 0)),
        ]
        + [pl.BlockSpec((1, SPAN, D), lambda x: (x, 0, 0))] * GROUPS,
        out_specs=pl.BlockSpec((1, RANK, D), lambda x: (x, 0, 0)),
        out_shape=jax.ShapeDtypeStruct((N_X, RANK, D), F32),
        compiler_params=pltpu.CompilerParams(vmem_limit_bytes=12 << 20),
        cost_estimate=pl.CostEstimate(flops=10**9, bytes_accessed=9 << 20, transcendentals=0),
        name="right",
    )(basis, hidden, order, *rows)


def spread_kernel(place_ref, rows_ref, out_ref):
    count = rows_ref.shape[0]
    pairs = place_ref.shape[0]
    pick = jnp.where(lax.broadcasted_iota(jnp.int32, (pairs, count), 1) == place_ref[...], 1.0, 0.0).astype(BF)
    out_ref[...] = dot(pick, rows_ref[...]).astype(BF).reshape(out_ref.shape)


def spread(place, rows):
    count = rows.shape[0]
    pairs = 256
    return pl.pallas_call(
        spread_kernel,
        grid=(TOK * 8 // pairs,),
        in_specs=[
            pl.BlockSpec((pairs, 1), lambda i: (i, 0)),
            pl.BlockSpec((count, FF), lambda i: (0, 0)),
        ],
        out_specs=pl.BlockSpec((pairs // 8, 8, FF), lambda i: (i, 0, 0)),
        out_shape=jax.ShapeDtypeStruct((TOK, 8, FF), BF),
        compiler_params=pltpu.CompilerParams(vmem_limit_bytes=16 << 20),
        cost_estimate=pl.CostEstimate(flops=2 * 10**9, bytes_accessed=4 << 20, transcendentals=0),
        name="spread",
    )(place, rows)


def turn(n, d):
    return [(i, (i + d) % n) for i in range(n)]


def places(expert_ids):
    ids = expert_ids
    hit = ids[:, :, None] == jnp.arange(N_X * N_Z, dtype=jnp.int32)[None, None, :]
    named = jnp.any(hit, axis=1)
    earlier = jnp.tril(jnp.ones((TOK, TOK), BF), -1)
    rank = dot(earlier, named.astype(BF))
    slot = jnp.sum(jnp.where(hit, rank[:, None, :], 0.0), axis=2).astype(jnp.int32)
    place = (ids % N_Z) * (N_X * CAP) + (ids // N_Z) * CAP + slot
    return place.reshape(TOK * 8, 1)


def basis_kernel(c_ref, mine_ref, other_ref, basis_ref):
    first = c_ref[0] == 0
    sums = []
    for x in range(N_X):
        mine, other = mine_ref[x], other_ref[x]
        sums.append(jnp.concatenate([jnp.where(first, mine, other), jnp.where(first, other, mine)], axis=0))
    exact = lax.Precision.HIGHEST
    gram = jnp.stack(
        [lax.dot_general(p, p, NT, precision=exact, preferred_element_type=F32) for p in sums]
    )
    shape = (N_X, RANK, RANK)
    row = lax.broadcasted_iota(jnp.int32, shape, 1)
    column = lax.broadcasted_iota(jnp.int32, shape, 2)
    done = jnp.where(row == column, 1.0, 0.0)
    for j in range(RANK):
        pivot = gram[:, j : j + 1, j : j + 1]
        below = jnp.where(row[:, :, :1] > j, gram[:, :, j : j + 1] / pivot, 0.0)
        scale = jnp.where(row[:, :, :1] == j, lax.rsqrt(pivot), 1.0)
        done = (done - below * done[:, j : j + 1, :]) * scale
        gram = gram - below * gram[:, j : j + 1, :]
    for x in range(N_X):
        basis_ref[x] = lax.dot_general(done[x], sums[x], NN, precision=exact, preferred_element_type=F32)


def orthonormal(c, mine, other):
    return pl.pallas_call(
        basis_kernel,
        in_specs=[pl.BlockSpec(memory_space=pltpu.SMEM)] + [pl.BlockSpec(memory_space=pltpu.VMEM)] * 2,
        out_shape=jax.ShapeDtypeStruct((N_X, RANK, FF), F32),
        compiler_params=pltpu.CompilerParams(vmem_limit_bytes=12 << 20),
        cost_estimate=pl.CostEstimate(flops=10**7, bytes_accessed=1 << 20, transcendentals=0),
        name="basis",
    )(c, mine, other)


def half_sum(parts, c):
    k = RANK // 2
    keep = lax.dynamic_slice_in_dim(parts, c * k, k, 1)
    send = lax.dynamic_slice_in_dim(parts, (1 - c) * k, k, 1)
    return keep + lax.ppermute(send, "c", turn(2, 1))


def ring_sum(a, axis):
    moved = [lax.ppermute(a, axis, turn(4, d)) for d in (2, 1, 3)]
    return a + moved[0] + (moved[1] + moved[2])


def sum_right(parts, x, c):
    half = half_sum(parts, c)
    total = lax.dynamic_index_in_dim(half, x, 0, keepdims=False)
    for d in (2, 1, 3):
        piece = lax.dynamic_index_in_dim(half, lax.rem(x + d, N_X), 0, keepdims=False)
        total = total + lax.ppermute(piece, "x", turn(N_X, d))
    total = ring_sum(total, "y")
    other = lax.ppermute(total, "c", turn(2, 1))
    return jnp.where(c == 0, jnp.concatenate([total, other]), jnp.concatenate([other, total]))


def shards(grad_out, expert_ids, gates, hidden, w_down, q_start):
    x, y, c, z = (lax.axis_index(name) for name in ("x", "y", "c", "z"))
    plane = ("x", "y", "c")
    at = z.reshape(1)
    k = RANK // N_REP
    rep = y * 2 + c
    warm = three_outside(lax.dynamic_slice(q_start[0].T, (rep * k, 0), (k, D)))
    warm = jnp.pad(warm, ((0, PAD - 3 * k), (0, 0)))
    gathered = lax.all_gather(jnp.concatenate([w_down[0], warm], axis=0), plane, axis=0, tiled=True)
    gathered = gathered.reshape(N_X, N_REP, SHARE + PAD, D)
    meta = jnp.concatenate([expert_ids.T.astype(F32), gates.T], axis=0)
    meta = lax.all_to_all(
        jnp.broadcast_to(meta[None], (N_Z,) + meta.shape), "z", split_axis=0, concat_axis=0, tiled=True
    )
    stored = lax.all_to_all(hidden.reshape(N_X, SLOTS, FF), "x", split_axis=0, concat_axis=0, tiled=True)

    blocks = [grad_out]
    right = left = grad_out
    rows = []
    for step in range(1, N_Z // 2):
        before = (right, left)
        right = lax.ppermute(right, "z", turn(N_Z, 1))
        left = lax.ppermute(left, "z", turn(N_Z, -1))
        beside = []
        if step == 1:
            beside = [meta]
        elif step == 2:
            picks, scale, order, move = make_picks(at, meta)
            beside = [picks]
        elif step == 3 or step == 5 or step == 7:
            g = len(rows)
            rows.append(make_rows(g, picks, scale, blocks[g * GROUP : (g + 1) * GROUP]))
            beside = [rows[g]]
        now = (right, left)
        right, _, *beside = lax.optimization_barrier((right, before[1], *beside))
        left, _ = lax.optimization_barrier((left, before[0]))
        if step == 1:
            meta = beside[0]
        blocks += [*now]
    half = TOK // 2
    last = blocks[12:] + [
        lax.ppermute(right[:half], "z", turn(N_Z, 1)),
        lax.ppermute(left[half:], "z", turn(N_Z, -1)),
    ]
    near = project(gathered, order, rows)
    last, near = lax.optimization_barrier((last, near))
    rows.append(make_rows(3, picks, scale, last))
    back = back_rows(at, gathered, move, rows)
    returned = lax.all_to_all(back, "z", split_axis=0, concat_axis=0, tiled=True)
    last_rows, _ = lax.optimization_barrier((rows[-1], back))
    p_half = half_sum(left_part(near, gathered, last_rows, stored, order), c)
    p_half = ring_sum(ring_sum(p_half, "y"), "x")
    basis = orthonormal(c.reshape(1), p_half, lax.ppermute(p_half, "c", turn(2, 1)))
    q_sum = sum_right(right_part(basis, stored, order, rows), x, c)
    p_basis = lax.dynamic_index_in_dim(basis, x, 0, keepdims=False).T * math.sqrt(FF)
    place = places(expert_ids)
    grad_hidden = spread(place, returned.reshape(N_Z * N_X * CAP, FF))
    return (grad_hidden, p_basis[None], (q_sum.T / N_REP)[None])


def solution(mesh):
    fine = Mesh(mesh.devices.reshape(N_Y, 2, N_X, N_Z), ("y", "c", "x", "z"))
    rep, exp = ("y", "c"), ("x", "z")
    in_specs = (
        P(rep + exp, None),
        P(rep + exp, None),
        P(rep + exp, None),
        P(rep, exp, None, None),
        P(exp, rep, None),
        P(exp, None, None),
    )
    out_specs = (P(rep + exp, None, None), P(exp, None, None), P(exp, None, None))
    return jax.shard_map(shards, mesh=fine, in_specs=in_specs, out_specs=out_specs, check_vma=False)
```

```python
import math

import jax
import jax.numpy as jnp
from jax import lax
from jax.experimental import pallas as pl
from jax.experimental.pallas import tpu as pltpu
from jax.sharding import Mesh
from jax.sharding import PartitionSpec as P

N_X = 4
N_Y = 4
N_Z = 16
N_REP = 8
CAP = 20
TOK = 128
D = 2048
FF = 768
RANK = 32
LIMIT = 56 << 20
GROUP = 4
GROUPS = N_Z // GROUP
SPAN = GROUP * CAP
SLOTS = N_Z * CAP
SHARE = FF // N_REP
PAD = 16
OFFSETS = [-((j + 1) // 2) if j % 2 else j // 2 for j in range(N_Z)]
BF = jnp.bfloat16
F32 = jnp.float32
NT = (((1,), (1,)), ((), ()))
NN = (((1,), (0,)), ((), ()))


def dot(a, b, dims=NN):
    return lax.dot_general(a, b, dims, preferred_element_type=F32)


def three(a):
    high = a.astype(BF)
    rest = a - high.astype(F32)
    mid = rest.astype(BF)
    low = (rest - mid.astype(F32)).astype(BF)
    return jnp.concatenate([high, mid, low], axis=0)


def three_outside(a):
    high = lax.reduce_precision(a, 8, 7)
    mid = lax.reduce_precision(a - high, 8, 7)
    return jnp.concatenate([high, mid, a - high - mid], axis=0).astype(BF)


def fold(a):
    n = a.shape[0] // 3
    return a[:n] + a[n : 2 * n] + a[2 * n :]


def offset(j):
    return jnp.where(j % 2 == 1, -((j + 1) // 2), j // 2)


def picks_kernel(z_ref, meta_ref, picks_ref, scale_ref, order_ref, move_ref):
    z = z_ref[0]
    earlier = (
        lax.broadcasted_iota(jnp.int32, (TOK, TOK), 0) < lax.broadcasted_iota(jnp.int32, (TOK, TOK), 1)
    ).astype(F32).astype(BF)
    slot_of = lax.broadcasted_iota(jnp.int32, (SPAN, TOK), 0).astype(F32)
    for g in range(GROUPS):
        named, gate = [], []
        for x in range(N_X):
            expert = (x * N_Z + z).astype(F32)
            for b in range(GROUP):
                at = lax.rem(z + OFFSETS[g * GROUP + b] + N_Z, N_Z)
                hit = meta_ref[at, 0:8, :] == expert
                named.append(jnp.sum(jnp.where(hit, 1.0, 0.0), axis=0, keepdims=True))
                gate.append(jnp.sum(jnp.where(hit, meta_ref[at, 8:16, :], 0.0), axis=0, keepdims=True))
        rank = dot(jnp.concatenate(named, axis=0).astype(BF), earlier)
        for x in range(N_X):
            scale = jnp.zeros((SPAN, 1), F32)
            for b in range(GROUP):
                i = x * GROUP + b
                target = jnp.where(named[i] > 0.5, rank[i : i + 1, :] + float(b * CAP), -1.0)
                hit = slot_of == target
                picks_ref[g, x * SPAN : (x + 1) * SPAN, b * TOK : (b + 1) * TOK] = jnp.where(hit, 1.0, 0.0).astype(BF)
                scale += jnp.sum(jnp.where(hit, gate[i], 0.0), axis=1, keepdims=True)
            scale_ref[g, x * SPAN : (x + 1) * SPAN, :] = jnp.broadcast_to(scale, (SPAN, 128))
    came = lax.broadcasted_iota(jnp.int32, (SLOTS, SLOTS), 0)
    own = lax.broadcasted_iota(jnp.int32, (SLOTS, SLOTS), 1)
    block = lax.rem(z + offset(came // CAP) + N_Z, N_Z)
    order_ref[...] = jnp.where(own == block * CAP + came % CAP, 1.0, 0.0).astype(BF)
    x, b, k = own // SPAN, (own % SPAN) // CAP, own % CAP
    move_ref[...] = jnp.where(came == b * (N_X * CAP) + x * CAP + k, 1.0, 0.0).astype(BF)


def make_picks(z, meta):
    slots = N_X * SPAN
    return pl.pallas_call(
        picks_kernel,
        in_specs=[pl.BlockSpec(memory_space=pltpu.SMEM), pl.BlockSpec(memory_space=pltpu.VMEM)],
        out_specs=[pl.BlockSpec(memory_space=pltpu.VMEM)] * 4,
        out_shape=[
            jax.ShapeDtypeStruct((GROUPS, slots, GROUP * TOK), BF),
            jax.ShapeDtypeStruct((GROUPS, slots, 128), F32),
            jax.ShapeDtypeStruct((SLOTS, SLOTS), BF),
            jax.ShapeDtypeStruct((SLOTS, SLOTS), BF),
        ],
        compiler_params=pltpu.CompilerParams(vmem_limit_bytes=LIMIT),
        cost_estimate=pl.CostEstimate(flops=10**7, bytes_accessed=4 << 20, transcendentals=0),
        name="picks",
    )(z, meta)


def rows_kernel(picks_ref, scale_ref, *refs):
    rows_ref = refs[-1]
    tokens = jnp.concatenate([ref[...] for ref in refs[:-1]], axis=0)
    for c in range(0, tokens.shape[1], 512):
        taken = dot(picks_ref[0], tokens[:, c : c + 512])
        for x in range(N_X):
            scale = scale_ref[0, x * SPAN : (x + 1) * SPAN, :1]
            rows_ref[x, :, c : c + 512] = (taken[x * SPAN : (x + 1) * SPAN] * scale).astype(BF)


def make_rows(group, picks, scale, blocks):
    slots = N_X * SPAN
    wide = D // 2
    return pl.pallas_call(
        rows_kernel,
        grid=(D // wide,),
        in_specs=[
            pl.BlockSpec((1, slots, GROUP * TOK), lambda i: (group, 0, 0)),
            pl.BlockSpec((1, slots, 128), lambda i: (group, 0, 0)),
        ]
        + [pl.BlockSpec((block.shape[0], wide), lambda i: (0, i)) for block in blocks],
        out_specs=pl.BlockSpec((N_X, SPAN, wide), lambda i: (0, 0, i)),
        out_shape=jax.ShapeDtypeStruct((N_X, SPAN, D), BF),
        compiler_params=pltpu.CompilerParams(vmem_limit_bytes=LIMIT),
        cost_estimate=pl.CostEstimate(flops=7 * 10**8, bytes_accessed=4 << 20, transcendentals=0),
        name="rows",
    )(picks, scale, *blocks)


def all_rows(refs):
    return jnp.concatenate([ref[0] for ref in refs], axis=0)


def unfold(a):
    a = a.reshape(N_REP, PAD, a.shape[1])
    k = RANK // N_REP
    return (a[:, :k] + a[:, k : 2 * k] + a[:, 2 * k : 3 * k]).reshape(RANK, a.shape[2])


def project_kernel(gathered_ref, order_ref, *refs):
    projected = unfold(dot(gathered_ref[0].reshape(N_REP * PAD, D), all_rows(refs[:-1]), NT))
    refs[-1][0] = dot(three(projected), order_ref[...]).astype(BF)


def project(gathered, order, rows):
    slots = len(rows) * SPAN
    return pl.pallas_call(
        project_kernel,
        grid=(N_X,),
        in_specs=[
            pl.BlockSpec((1, N_REP, PAD, D), lambda x: (x, 0, SHARE // PAD, 0)),
            pl.BlockSpec((slots, SLOTS), lambda x: (0, 0)),
        ]
        + [pl.BlockSpec((1, SPAN, D), lambda x: (x, 0, 0))] * len(rows),
        out_specs=pl.BlockSpec((1, 3 * RANK, SLOTS), lambda x: (x, 0, 0)),
        out_shape=jax.ShapeDtypeStruct((N_X, 3 * RANK, SLOTS), BF),
        compiler_params=pltpu.CompilerParams(vmem_limit_bytes=LIMIT),
        cost_estimate=pl.CostEstimate(flops=10**9, bytes_accessed=6 << 20, transcendentals=0),
        name="project",
    )(gathered, order, *rows)


def left_kernel(near_ref, gathered_ref, rows_ref, hidden_ref, order_ref, part_ref):
    projected = unfold(dot(gathered_ref[0].reshape(N_REP * PAD, D), rows_ref[0], NT))
    ordered = near_ref[0] + dot(three(projected), order_ref[...]).astype(BF)
    part_ref[0] = fold(dot(ordered, hidden_ref[0]))


def left_part(near, gathered, rows, hidden, order):
    last = GROUPS - 1
    return pl.pallas_call(
        left_kernel,
        grid=(N_X,),
        in_specs=[
            pl.BlockSpec((1, 3 * RANK, SLOTS), lambda x: (x, 0, 0)),
            pl.BlockSpec((1, N_REP, PAD, D), lambda x: (x, 0, SHARE // PAD, 0)),
            pl.BlockSpec((1, SPAN, D), lambda x: (x, 0, 0)),
            pl.BlockSpec((1, SLOTS, FF), lambda x: (x, 0, 0)),
            pl.BlockSpec((SPAN, SLOTS), lambda x: (last, 0)),
        ],
        out_specs=pl.BlockSpec((1, RANK, FF), lambda x: (x, 0, 0)),
        out_shape=jax.ShapeDtypeStruct((N_X, RANK, FF), F32),
        compiler_params=pltpu.CompilerParams(vmem_limit_bytes=LIMIT),
        cost_estimate=pl.CostEstimate(flops=10**9, bytes_accessed=6 << 20, transcendentals=0),
        name="left",
    )(near, gathered, rows, hidden, order)


def back_kernel(z_ref, gathered_ref, move_ref, *refs):
    back_ref, held_ref = refs[-2:]
    x = pl.program_id(0)
    z = z_ref[0]
    weight = gathered_ref[0, :, :SHARE, :].reshape(FF, D)
    rows = all_rows(refs[:-2])
    for c in range(0, FF, 256):
        held_ref[pl.ds(x, 1), :, c : c + 256] = dot(rows, weight[c : c + 256], NT).astype(BF)[None]

    @pl.when(x == N_X - 1)
    def _():
        for g in range(GROUPS):
            source = jnp.concatenate([held_ref[i, g * SPAN : (g + 1) * SPAN, :] for i in range(N_X)], axis=0)
            moved = dot(move_ref[...], source).astype(BF)
            for b in range(GROUP):
                at = lax.rem(z + OFFSETS[g * GROUP + b] + N_Z, N_Z)
                back_ref[pl.ds(at, 1)] = moved[b * N_X * CAP : (b + 1) * N_X * CAP][None]


def back_rows(z, gathered, move, rows):
    return pl.pallas_call(
        back_kernel,
        grid_spec=pltpu.PrefetchScalarGridSpec(
            num_scalar_prefetch=1,
            grid=(N_X,),
            in_specs=[
                pl.BlockSpec((1, N_REP, SHARE + PAD, D), lambda x, s: (x, 0, 0, 0)),
                pl.BlockSpec((SLOTS, SLOTS), lambda x, s: (0, 0)),
            ]
            + [pl.BlockSpec((1, SPAN, D), lambda x, s: (x, 0, 0))] * GROUPS,
            out_specs=pl.BlockSpec((N_Z, N_X * CAP, FF), lambda x, s: (0, 0, 0)),
            scratch_shapes=[pltpu.VMEM((N_X, SLOTS, FF), BF)],
        ),
        out_shape=jax.ShapeDtypeStruct((N_Z, N_X * CAP, FF), BF),
        compiler_params=pltpu.CompilerParams(vmem_limit_bytes=LIMIT),
        cost_estimate=pl.CostEstimate(flops=4 * 10**9, bytes_accessed=20 << 20, transcendentals=0),
        name="back",
    )(z, gathered, move, *rows)


def right_kernel(basis_ref, hidden_ref, order_ref, *refs):
    part_ref = refs[-1]
    mapped = fold(dot(three(basis_ref[0]), hidden_ref[0], NT))
    ordered = dot(three(mapped), order_ref[...], NT).astype(BF)
    part_ref[0] = fold(dot(ordered, all_rows(refs[:-1])))


def right_part(basis, hidden, order, rows):
    return pl.pallas_call(
        right_kernel,
        grid=(N_X,),
        in_specs=[
            pl.BlockSpec((1, RANK, FF), lambda x: (x, 0, 0)),
            pl.BlockSpec((1, SLOTS, FF), lambda x: (x, 0, 0)),
            pl.BlockSpec((SLOTS, SLOTS), lambda x: (0, 0)),
        ]
        + [pl.BlockSpec((1, SPAN, D), lambda x: (x, 0, 0))] * GROUPS,
        out_specs=pl.BlockSpec((1, RANK, D), lambda x: (x, 0, 0)),
        out_shape=jax.ShapeDtypeStruct((N_X, RANK, D), F32),
        compiler_params=pltpu.CompilerParams(vmem_limit_bytes=12 << 20),
        cost_estimate=pl.CostEstimate(flops=10**9, bytes_accessed=9 << 20, transcendentals=0),
        name="right",
    )(basis, hidden, order, *rows)


def spread_kernel(place_ref, rows_ref, out_ref):
    count = rows_ref.shape[0]
    pairs = place_ref.shape[0]
    pick = jnp.where(lax.broadcasted_iota(jnp.int32, (pairs, count), 1) == place_ref[...], 1.0, 0.0).astype(BF)
    out_ref[...] = dot(pick, rows_ref[...]).astype(BF).reshape(out_ref.shape)


def spread(place, rows):
    count = rows.shape[0]
    pairs = 256
    return pl.pallas_call(
        spread_kernel,
        grid=(TOK * 8 // pairs,),
        in_specs=[
            pl.BlockSpec((pairs, 1), lambda i: (i, 0)),
            pl.BlockSpec((count, FF), lambda i: (0, 0)),
        ],
        out_specs=pl.BlockSpec((pairs // 8, 8, FF), lambda i: (i, 0, 0)),
        out_shape=jax.ShapeDtypeStruct((TOK, 8, FF), BF),
        compiler_params=pltpu.CompilerParams(vmem_limit_bytes=16 << 20),
        cost_estimate=pl.CostEstimate(flops=2 * 10**9, bytes_accessed=4 << 20, transcendentals=0),
        name="spread",
    )(place, rows)


def turn(n, d):
    return [(i, (i + d) % n) for i in range(n)]


def places(expert_ids):
    ids = expert_ids
    hit = ids[:, :, None] == jnp.arange(N_X * N_Z, dtype=jnp.int32)[None, None, :]
    named = jnp.any(hit, axis=1)
    earlier = jnp.tril(jnp.ones((TOK, TOK), BF), -1)
    rank = dot(earlier, named.astype(BF))
    slot = jnp.sum(jnp.where(hit, rank[:, None, :], 0.0), axis=2).astype(jnp.int32)
    place = (ids % N_Z) * (N_X * CAP) + (ids // N_Z) * CAP + slot
    return place.reshape(TOK * 8, 1)


def basis_kernel(c_ref, mine_ref, other_ref, basis_ref):
    first = c_ref[0] == 0
    sums = []
    for x in range(N_X):
        mine, other = mine_ref[x], other_ref[x]
        sums.append(jnp.concatenate([jnp.where(first, mine, other), jnp.where(first, other, mine)], axis=0))
    exact = lax.Precision.HIGHEST
    gram = jnp.stack(
        [lax.dot_general(p, p, NT, precision=exact, preferred_element_type=F32) for p in sums]
    )
    shape = (N_X, RANK, RANK)
    row = lax.broadcasted_iota(jnp.int32, shape, 1)
    column = lax.broadcasted_iota(jnp.int32, shape, 2)
    done = jnp.where(row == column, 1.0, 0.0)
    for j in range(RANK):
        pivot = gram[:, j : j + 1, j : j + 1]
        below = jnp.where(row[:, :, :1] > j, gram[:, :, j : j + 1] / pivot, 0.0)
        scale = jnp.where(row[:, :, :1] == j, lax.rsqrt(pivot), 1.0)
        done = (done - below * done[:, j : j + 1, :]) * scale
        gram = gram - below * gram[:, j : j + 1, :]
    for x in range(N_X):
        basis_ref[x] = lax.dot_general(done[x], sums[x], NN, precision=exact, preferred_element_type=F32)


def orthonormal(c, mine, other):
    return pl.pallas_call(
        basis_kernel,
        in_specs=[pl.BlockSpec(memory_space=pltpu.SMEM)] + [pl.BlockSpec(memory_space=pltpu.VMEM)] * 2,
        out_shape=jax.ShapeDtypeStruct((N_X, RANK, FF), F32),
        compiler_params=pltpu.CompilerParams(vmem_limit_bytes=12 << 20),
        cost_estimate=pl.CostEstimate(flops=10**7, bytes_accessed=1 << 20, transcendentals=0),
        name="basis",
    )(c, mine, other)


def half_sum(parts, c):
    k = RANK // 2
    keep = lax.dynamic_slice_in_dim(parts, c * k, k, 1)
    send = lax.dynamic_slice_in_dim(parts, (1 - c) * k, k, 1)
    return keep + lax.ppermute(send, "c", turn(2, 1))


def ring_sum(a, axis):
    moved = [lax.ppermute(a, axis, turn(4, d)) for d in (2, 1, 3)]
    return a + moved[0] + (moved[1] + moved[2])


def sum_right(parts, x, c):
    half = half_sum(parts, c)
    total = lax.dynamic_index_in_dim(half, x, 0, keepdims=False)
    for d in (2, 1, 3):
        piece = lax.dynamic_index_in_dim(half, lax.rem(x + d, N_X), 0, keepdims=False)
        total = total + lax.ppermute(piece, "x", turn(N_X, d))
    total = ring_sum(total, "y")
    other = lax.ppermute(total, "c", turn(2, 1))
    return jnp.where(c == 0, jnp.concatenate([total, other]), jnp.concatenate([other, total]))


def shards(grad_out, expert_ids, gates, hidden, w_down, q_start):
    x, y, c, z = (lax.axis_index(name) for name in ("x", "y", "c", "z"))
    plane = ("x", "y", "c")
    at = z.reshape(1)
    k = RANK // N_REP
    rep = y * 2 + c
    warm = three_outside(lax.dynamic_slice(q_start[0].T, (rep * k, 0), (k, D)))
    warm = jnp.pad(warm, ((0, PAD - 3 * k), (0, 0)))
    gathered = lax.all_gather(jnp.concatenate([w_down[0], warm], axis=0), plane, axis=0, tiled=True)
    gathered = gathered.reshape(N_X, N_REP, SHARE + PAD, D)
    meta = jnp.concatenate([expert_ids.T.astype(F32), gates.T], axis=0)
    meta = lax.all_to_all(
        jnp.broadcast_to(meta[None], (N_Z,) + meta.shape), "z", split_axis=0, concat_axis=0, tiled=True
    )
    stored = lax.all_to_all(hidden.reshape(N_X, SLOTS, FF), "x", split_axis=0, concat_axis=0, tiled=True)

    blocks = [grad_out]
    right = left = grad_out
    rows = []
    for step in range(1, N_Z // 2):
        before = (right, left)
        right = lax.ppermute(right, "z", turn(N_Z, 1))
        left = lax.ppermute(left, "z", turn(N_Z, -1))
        beside = []
        if step == 1:
            beside = [meta]
        elif step == 2:
            picks, scale, order, move = make_picks(at, meta)
            beside = [picks]
        elif step == 3 or step == 5 or step == 7:
            g = len(rows)
            rows.append(make_rows(g, picks, scale, blocks[g * GROUP : (g + 1) * GROUP]))
            beside = [rows[g]]
        now = (right, left)
        if step < 6:
            right, _, *beside = lax.optimization_barrier((right, before[1], *beside))
            left, _ = lax.optimization_barrier((left, before[0]))
        else:
            right, left, *beside = lax.optimization_barrier((right, left, *beside))
        if step == 1:
            meta = beside[0]
        blocks += [*now]
    half = TOK // 2
    last = blocks[12:] + [
        lax.ppermute(right[:half], "z", turn(N_Z, 1)),
        lax.ppermute(left[half:], "z", turn(N_Z, -1)),
    ]
    near = project(gathered, order, rows)
    last, near = lax.optimization_barrier((last, near))
    rows.append(make_rows(3, picks, scale, last))
    back = back_rows(at, gathered, move, rows)
    returned = lax.all_to_all(back, "z", split_axis=0, concat_axis=0, tiled=True)
    last_rows, _ = lax.optimization_barrier((rows[-1], back))
    p_half = half_sum(left_part(near, gathered, last_rows, stored, order), c)
    p_half = ring_sum(ring_sum(p_half, "y"), "x")
    basis = orthonormal(c.reshape(1), p_half, lax.ppermute(p_half, "c", turn(2, 1)))
    q_sum = sum_right(right_part(basis, stored, order, rows), x, c)
    p_basis = lax.dynamic_index_in_dim(basis, x, 0, keepdims=False).T * math.sqrt(FF)
    place = places(expert_ids)
    grad_hidden = spread(place, returned.reshape(N_Z * N_X * CAP, FF))
    return (grad_hidden, p_basis[None], (q_sum.T / N_REP)[None])


def solution(mesh):
    fine = Mesh(mesh.devices.reshape(N_Y, 2, N_X, N_Z), ("y", "c", "x", "z"))
    rep, exp = ("y", "c"), ("x", "z")
    in_specs = (
        P(rep + exp, None),
        P(rep + exp, None),
        P(rep + exp, None),
        P(rep, exp, None, None),
        P(exp, rep, None),
        P(exp, None, None),
    )
    out_specs = (P(rep + exp, None, None), P(exp, None, None), P(exp, None, None))
    return jax.shard_map(shards, mesh=fine, in_specs=in_specs, out_specs=out_specs, check_vma=False)
```

```python
import math

import jax
import jax.numpy as jnp
from jax import lax
from jax.experimental import pallas as pl
from jax.experimental.pallas import tpu as pltpu
from jax.sharding import Mesh
from jax.sharding import PartitionSpec as P

N_X = 4
N_Y = 4
N_Z = 16
N_REP = 8
CAP = 20
TOK = 128
D = 2048
FF = 768
RANK = 32
LIMIT = 56 << 20
GROUP = 4
GROUPS = N_Z // GROUP
SPAN = GROUP * CAP
SLOTS = N_Z * CAP
SHARE = FF // N_REP
PAD = 16
OFFSETS = [-((j + 1) // 2) if j % 2 else j // 2 for j in range(N_Z)]
BF = jnp.bfloat16
F32 = jnp.float32
NT = (((1,), (1,)), ((), ()))
NN = (((1,), (0,)), ((), ()))


def dot(a, b, dims=NN):
    return lax.dot_general(a, b, dims, preferred_element_type=F32)


def three(a):
    high = a.astype(BF)
    rest = a - high.astype(F32)
    mid = rest.astype(BF)
    low = (rest - mid.astype(F32)).astype(BF)
    return jnp.concatenate([high, mid, low], axis=0)


def three_outside(a):
    high = lax.reduce_precision(a, 8, 7)
    mid = lax.reduce_precision(a - high, 8, 7)
    return jnp.concatenate([high, mid, a - high - mid], axis=0).astype(BF)


def fold(a):
    n = a.shape[0] // 3
    return a[:n] + a[n : 2 * n] + a[2 * n :]


def offset(j):
    return jnp.where(j % 2 == 1, -((j + 1) // 2), j // 2)


def picks_kernel(z_ref, meta_ref, picks_ref, scale_ref, order_ref, move_ref):
    z = z_ref[0]
    earlier = (
        lax.broadcasted_iota(jnp.int32, (TOK, TOK), 0) < lax.broadcasted_iota(jnp.int32, (TOK, TOK), 1)
    ).astype(F32).astype(BF)
    slot_of = lax.broadcasted_iota(jnp.int32, (SPAN, TOK), 0).astype(F32)
    for g in range(GROUPS):
        named, gate = [], []
        for x in range(N_X):
            expert = (x * N_Z + z).astype(F32)
            for b in range(GROUP):
                at = lax.rem(z + OFFSETS[g * GROUP + b] + N_Z, N_Z)
                hit = meta_ref[at, 0:8, :] == expert
                named.append(jnp.sum(jnp.where(hit, 1.0, 0.0), axis=0, keepdims=True))
                gate.append(jnp.sum(jnp.where(hit, meta_ref[at, 8:16, :], 0.0), axis=0, keepdims=True))
        rank = dot(jnp.concatenate(named, axis=0).astype(BF), earlier)
        for x in range(N_X):
            scale = jnp.zeros((SPAN, 1), F32)
            for b in range(GROUP):
                i = x * GROUP + b
                target = jnp.where(named[i] > 0.5, rank[i : i + 1, :] + float(b * CAP), -1.0)
                hit = slot_of == target
                picks_ref[g, x * SPAN : (x + 1) * SPAN, b * TOK : (b + 1) * TOK] = jnp.where(hit, 1.0, 0.0).astype(BF)
                scale += jnp.sum(jnp.where(hit, gate[i], 0.0), axis=1, keepdims=True)
            scale_ref[g, x * SPAN : (x + 1) * SPAN, :] = jnp.broadcast_to(scale, (SPAN, 128))
    came = lax.broadcasted_iota(jnp.int32, (SLOTS, SLOTS), 0)
    own = lax.broadcasted_iota(jnp.int32, (SLOTS, SLOTS), 1)
    block = lax.rem(z + offset(came // CAP) + N_Z, N_Z)
    order_ref[...] = jnp.where(own == block * CAP + came % CAP, 1.0, 0.0).astype(BF)
    x, b, k = own // SPAN, (own % SPAN) // CAP, own % CAP
    move_ref[...] = jnp.where(came == b * (N_X * CAP) + x * CAP + k, 1.0, 0.0).astype(BF)


def make_picks(z, meta):
    slots = N_X * SPAN
    return pl.pallas_call(
        picks_kernel,
        in_specs=[pl.BlockSpec(memory_space=pltpu.SMEM), pl.BlockSpec(memory_space=pltpu.VMEM)],
        out_specs=[pl.BlockSpec(memory_space=pltpu.VMEM)] * 4,
        out_shape=[
            jax.ShapeDtypeStruct((GROUPS, slots, GROUP * TOK), BF),
            jax.ShapeDtypeStruct((GROUPS, slots, 128), F32),
            jax.ShapeDtypeStruct((SLOTS, SLOTS), BF),
            jax.ShapeDtypeStruct((SLOTS, SLOTS), BF),
        ],
        compiler_params=pltpu.CompilerParams(vmem_limit_bytes=LIMIT),
        cost_estimate=pl.CostEstimate(flops=10**7, bytes_accessed=4 << 20, transcendentals=0),
        name="picks",
    )(z, meta)


def rows_kernel(picks_ref, scale_ref, *refs):
    rows_ref = refs[-1]
    tokens = jnp.concatenate([ref[...] for ref in refs[:-1]], axis=0)
    for c in range(0, tokens.shape[1], 512):
        taken = dot(picks_ref[0], tokens[:, c : c + 512])
        for x in range(N_X):
            scale = scale_ref[0, x * SPAN : (x + 1) * SPAN, :1]
            rows_ref[x, :, c : c + 512] = (taken[x * SPAN : (x + 1) * SPAN] * scale).astype(BF)


def make_rows(group, picks, scale, blocks):
    slots = N_X * SPAN
    wide = D // 2
    return pl.pallas_call(
        rows_kernel,
        grid=(D // wide,),
        in_specs=[
            pl.BlockSpec((1, slots, GROUP * TOK), lambda i: (group, 0, 0)),
            pl.BlockSpec((1, slots, 128), lambda i: (group, 0, 0)),
        ]
        + [pl.BlockSpec((block.shape[0], wide), lambda i: (0, i)) for block in blocks],
        out_specs=pl.BlockSpec((N_X, SPAN, wide), lambda i: (0, 0, i)),
        out_shape=jax.ShapeDtypeStruct((N_X, SPAN, D), BF),
        compiler_params=pltpu.CompilerParams(vmem_limit_bytes=LIMIT),
        cost_estimate=pl.CostEstimate(flops=7 * 10**8, bytes_accessed=4 << 20, transcendentals=0),
        name="rows",
    )(picks, scale, *blocks)


def all_rows(refs):
    return jnp.concatenate([ref[0] for ref in refs], axis=0)


def unfold(a):
    a = a.reshape(N_REP, PAD, a.shape[1])
    k = RANK // N_REP
    return (a[:, :k] + a[:, k : 2 * k] + a[:, 2 * k : 3 * k]).reshape(RANK, a.shape[2])


def project_kernel(gathered_ref, order_ref, *refs):
    projected = unfold(dot(gathered_ref[0].reshape(N_REP * PAD, D), all_rows(refs[:-1]), NT))
    refs[-1][0] = dot(three(projected), order_ref[...]).astype(BF)


def project(gathered, order, rows):
    slots = len(rows) * SPAN
    return pl.pallas_call(
        project_kernel,
        grid=(N_X,),
        in_specs=[
            pl.BlockSpec((1, N_REP, PAD, D), lambda x: (x, 0, SHARE // PAD, 0)),
            pl.BlockSpec((slots, SLOTS), lambda x: (0, 0)),
        ]
        + [pl.BlockSpec((1, SPAN, D), lambda x: (x, 0, 0))] * len(rows),
        out_specs=pl.BlockSpec((1, 3 * RANK, SLOTS), lambda x: (x, 0, 0)),
        out_shape=jax.ShapeDtypeStruct((N_X, 3 * RANK, SLOTS), BF),
        compiler_params=pltpu.CompilerParams(vmem_limit_bytes=LIMIT),
        cost_estimate=pl.CostEstimate(flops=10**9, bytes_accessed=6 << 20, transcendentals=0),
        name="project",
    )(gathered, order, *rows)


def left_kernel(near_ref, gathered_ref, rows_ref, hidden_ref, order_ref, part_ref):
    projected = unfold(dot(gathered_ref[0].reshape(N_REP * PAD, D), rows_ref[0], NT))
    ordered = near_ref[0] + dot(three(projected), order_ref[...]).astype(BF)
    part_ref[0] = fold(dot(ordered, hidden_ref[0]))


def left_part(near, gathered, rows, hidden, order):
    last = GROUPS - 1
    return pl.pallas_call(
        left_kernel,
        grid=(N_X,),
        in_specs=[
            pl.BlockSpec((1, 3 * RANK, SLOTS), lambda x: (x, 0, 0)),
            pl.BlockSpec((1, N_REP, PAD, D), lambda x: (x, 0, SHARE // PAD, 0)),
            pl.BlockSpec((1, SPAN, D), lambda x: (x, 0, 0)),
            pl.BlockSpec((1, SLOTS, FF), lambda x: (x, 0, 0)),
            pl.BlockSpec((SPAN, SLOTS), lambda x: (last, 0)),
        ],
        out_specs=pl.BlockSpec((1, RANK, FF), lambda x: (x, 0, 0)),
        out_shape=jax.ShapeDtypeStruct((N_X, RANK, FF), F32),
        compiler_params=pltpu.CompilerParams(vmem_limit_bytes=LIMIT),
        cost_estimate=pl.CostEstimate(flops=10**9, bytes_accessed=6 << 20, transcendentals=0),
        name="left",
    )(near, gathered, rows, hidden, order)


def back_kernel(z_ref, gathered_ref, move_ref, *refs):
    back_ref, held_ref = refs[-2:]
    x = pl.program_id(0)
    z = z_ref[0]
    weight = gathered_ref[0, :, :SHARE, :].reshape(FF, D)
    rows = all_rows(refs[:-2])
    for c in range(0, FF, 256):
        held_ref[pl.ds(x, 1), :, c : c + 256] = dot(rows, weight[c : c + 256], NT).astype(BF)[None]

    @pl.when(x == N_X - 1)
    def _():
        for g in range(GROUPS):
            source = jnp.concatenate([held_ref[i, g * SPAN : (g + 1) * SPAN, :] for i in range(N_X)], axis=0)
            moved = dot(move_ref[...], source).astype(BF)
            for b in range(GROUP):
                at = lax.rem(z + OFFSETS[g * GROUP + b] + N_Z, N_Z)
                back_ref[pl.ds(at, 1)] = moved[b * N_X * CAP : (b + 1) * N_X * CAP][None]


def back_rows(z, gathered, move, rows):
    return pl.pallas_call(
        back_kernel,
        grid_spec=pltpu.PrefetchScalarGridSpec(
            num_scalar_prefetch=1,
            grid=(N_X,),
            in_specs=[
                pl.BlockSpec((1, N_REP, SHARE + PAD, D), lambda x, s: (x, 0, 0, 0)),
                pl.BlockSpec((SLOTS, SLOTS), lambda x, s: (0, 0)),
            ]
            + [pl.BlockSpec((1, SPAN, D), lambda x, s: (x, 0, 0))] * GROUPS,
            out_specs=pl.BlockSpec((N_Z, N_X * CAP, FF), lambda x, s: (0, 0, 0)),
            scratch_shapes=[pltpu.VMEM((N_X, SLOTS, FF), BF)],
        ),
        out_shape=jax.ShapeDtypeStruct((N_Z, N_X * CAP, FF), BF),
        compiler_params=pltpu.CompilerParams(vmem_limit_bytes=LIMIT),
        cost_estimate=pl.CostEstimate(flops=4 * 10**9, bytes_accessed=20 << 20, transcendentals=0),
        name="back",
    )(z, gathered, move, *rows)


def right_kernel(basis_ref, hidden_ref, order_ref, *refs):
    part_ref = refs[-1]
    mapped = fold(dot(three(basis_ref[0]), hidden_ref[0], NT))
    ordered = dot(three(mapped), order_ref[...], NT).astype(BF)
    part_ref[0] = fold(dot(ordered, all_rows(refs[:-1])))


def right_part(basis, hidden, order, rows):
    return pl.pallas_call(
        right_kernel,
        grid=(N_X,),
        in_specs=[
            pl.BlockSpec((1, RANK, FF), lambda x: (x, 0, 0)),
            pl.BlockSpec((1, SLOTS, FF), lambda x: (x, 0, 0)),
            pl.BlockSpec((SLOTS, SLOTS), lambda x: (0, 0)),
        ]
        + [pl.BlockSpec((1, SPAN, D), lambda x: (x, 0, 0))] * GROUPS,
        out_specs=pl.BlockSpec((1, RANK, D), lambda x: (x, 0, 0)),
        out_shape=jax.ShapeDtypeStruct((N_X, RANK, D), F32),
        compiler_params=pltpu.CompilerParams(vmem_limit_bytes=12 << 20),
        cost_estimate=pl.CostEstimate(flops=10**9, bytes_accessed=9 << 20, transcendentals=0),
        name="right",
    )(basis, hidden, order, *rows)


def spread_kernel(place_ref, rows_ref, out_ref):
    count = rows_ref.shape[0]
    pairs = place_ref.shape[0]
    pick = jnp.where(lax.broadcasted_iota(jnp.int32, (pairs, count), 1) == place_ref[...], 1.0, 0.0).astype(BF)
    out_ref[...] = dot(pick, rows_ref[...]).astype(BF).reshape(out_ref.shape)


def spread(place, rows):
    count = rows.shape[0]
    pairs = 256
    return pl.pallas_call(
        spread_kernel,
        grid=(TOK * 8 // pairs,),
        in_specs=[
            pl.BlockSpec((pairs, 1), lambda i: (i, 0)),
            pl.BlockSpec((count, FF), lambda i: (0, 0)),
        ],
        out_specs=pl.BlockSpec((pairs // 8, 8, FF), lambda i: (i, 0, 0)),
        out_shape=jax.ShapeDtypeStruct((TOK, 8, FF), BF),
        compiler_params=pltpu.CompilerParams(vmem_limit_bytes=16 << 20),
        cost_estimate=pl.CostEstimate(flops=2 * 10**9, bytes_accessed=4 << 20, transcendentals=0),
        name="spread",
    )(place, rows)


def turn(n, d):
    return [(i, (i + d) % n) for i in range(n)]


def places(expert_ids):
    ids = expert_ids
    hit = ids[:, :, None] == jnp.arange(N_X * N_Z, dtype=jnp.int32)[None, None, :]
    named = jnp.any(hit, axis=1)
    earlier = jnp.tril(jnp.ones((TOK, TOK), BF), -1)
    rank = dot(earlier, named.astype(BF))
    slot = jnp.sum(jnp.where(hit, rank[:, None, :], 0.0), axis=2).astype(jnp.int32)
    place = (ids % N_Z) * (N_X * CAP) + (ids // N_Z) * CAP + slot
    return place.reshape(TOK * 8, 1)


def basis_kernel(c_ref, mine_ref, other_ref, basis_ref):
    first = c_ref[0] == 0
    sums = []
    for x in range(N_X):
        mine, other = mine_ref[x], other_ref[x]
        sums.append(jnp.concatenate([jnp.where(first, mine, other), jnp.where(first, other, mine)], axis=0))
    exact = lax.Precision.HIGHEST
    gram = jnp.stack(
        [lax.dot_general(p, p, NT, precision=exact, preferred_element_type=F32) for p in sums]
    )
    shape = (N_X, RANK, RANK)
    row = lax.broadcasted_iota(jnp.int32, shape, 1)
    column = lax.broadcasted_iota(jnp.int32, shape, 2)
    done = jnp.where(row == column, 1.0, 0.0)
    for j in range(RANK):
        pivot = gram[:, j : j + 1, j : j + 1]
        below = jnp.where(row[:, :, :1] > j, gram[:, :, j : j + 1] / pivot, 0.0)
        scale = jnp.where(row[:, :, :1] == j, lax.rsqrt(pivot), 1.0)
        done = (done - below * done[:, j : j + 1, :]) * scale
        gram = gram - below * gram[:, j : j + 1, :]
    for x in range(N_X):
        basis_ref[x] = lax.dot_general(done[x], sums[x], NN, precision=exact, preferred_element_type=F32)


def orthonormal(c, mine, other):
    return pl.pallas_call(
        basis_kernel,
        in_specs=[pl.BlockSpec(memory_space=pltpu.SMEM)] + [pl.BlockSpec(memory_space=pltpu.VMEM)] * 2,
        out_shape=jax.ShapeDtypeStruct((N_X, RANK, FF), F32),
        compiler_params=pltpu.CompilerParams(vmem_limit_bytes=12 << 20),
        cost_estimate=pl.CostEstimate(flops=10**7, bytes_accessed=1 << 20, transcendentals=0),
        name="basis",
    )(c, mine, other)


def half_sum(parts, c):
    k = RANK // 2
    keep = lax.dynamic_slice_in_dim(parts, c * k, k, 1)
    send = lax.dynamic_slice_in_dim(parts, (1 - c) * k, k, 1)
    return keep + lax.ppermute(send, "c", turn(2, 1))


def ring_sum(a, axis):
    moved = [lax.ppermute(a, axis, turn(4, d)) for d in (2, 1, 3)]
    return a + moved[0] + (moved[1] + moved[2])


def sum_right(parts, x, c, beside):
    half = half_sum(parts, c)
    total = lax.dynamic_index_in_dim(half, x, 0, keepdims=False)
    for d in (2, 1, 3):
        piece = lax.dynamic_index_in_dim(half, lax.rem(x + d, N_X), 0, keepdims=False)
        total = total + lax.ppermute(piece, "x", turn(N_X, d))
    moved = [lax.ppermute(total, "y", turn(N_Y, d)) for d in (2, 1, 3)]
    beside = beside()
    moved, beside = lax.optimization_barrier((moved, beside))
    total = total + moved[0] + (moved[1] + moved[2])
    other = lax.ppermute(total, "c", turn(2, 1))
    whole = jnp.where(c == 0, jnp.concatenate([total, other]), jnp.concatenate([other, total]))
    return whole, beside


def shards(grad_out, expert_ids, gates, hidden, w_down, q_start):
    x, y, c, z = (lax.axis_index(name) for name in ("x", "y", "c", "z"))
    plane = ("x", "y", "c")
    at = z.reshape(1)
    k = RANK // N_REP
    rep = y * 2 + c
    warm = three_outside(lax.dynamic_slice(q_start[0].T, (rep * k, 0), (k, D)))
    warm = jnp.pad(warm, ((0, PAD - 3 * k), (0, 0)))
    gathered = lax.all_gather(jnp.concatenate([w_down[0], warm], axis=0), plane, axis=0, tiled=True)
    gathered = gathered.reshape(N_X, N_REP, SHARE + PAD, D)
    meta = jnp.concatenate([expert_ids.T.astype(F32), gates.T], axis=0)
    meta = lax.all_to_all(
        jnp.broadcast_to(meta[None], (N_Z,) + meta.shape), "z", split_axis=0, concat_axis=0, tiled=True
    )
    stored = lax.all_to_all(hidden.reshape(N_X, SLOTS, FF), "x", split_axis=0, concat_axis=0, tiled=True)

    blocks = [grad_out]
    right = left = grad_out
    rows = []
    for step in range(1, N_Z // 2):
        before = (right, left)
        right = lax.ppermute(right, "z", turn(N_Z, 1))
        left = lax.ppermute(left, "z", turn(N_Z, -1))
        beside = []
        if step == 1:
            beside = [meta]
        elif step == 2:
            picks, scale, order, move = make_picks(at, meta)
            beside = [picks]
        elif step == 3 or step == 5 or step == 7:
            g = len(rows)
            rows.append(make_rows(g, picks, scale, blocks[g * GROUP : (g + 1) * GROUP]))
            beside = [rows[g]]
        now = (right, left)
        if step < 6:
            right, _, *beside = lax.optimization_barrier((right, before[1], *beside))
            left, _ = lax.optimization_barrier((left, before[0]))
        else:
            right, left, *beside = lax.optimization_barrier((right, left, *beside))
        if step == 1:
            meta = beside[0]
        blocks += [*now]
    half = TOK // 2
    last = blocks[12:] + [
        lax.ppermute(right[:half], "z", turn(N_Z, 1)),
        lax.ppermute(left[half:], "z", turn(N_Z, -1)),
    ]
    near = project(gathered, order, rows)
    last, near = lax.optimization_barrier((last, near))
    rows.append(make_rows(3, picks, scale, last))
    back = back_rows(at, gathered, move, rows)
    returned = lax.all_to_all(back, "z", split_axis=0, concat_axis=0, tiled=True)
    last_rows, _ = lax.optimization_barrier((rows[-1], back))
    p_half = half_sum(left_part(near, gathered, last_rows, stored, order), c)
    p_half = ring_sum(ring_sum(p_half, "y"), "x")
    basis = orthonormal(c.reshape(1), p_half, lax.ppermute(p_half, "c", turn(2, 1)))
    place = places(expert_ids)
    q_sum, grad_hidden = sum_right(
        right_part(basis, stored, order, rows),
        x,
        c,
        lambda: spread(place, returned.reshape(N_Z * N_X * CAP, FF)),
    )
    p_basis = lax.dynamic_index_in_dim(basis, x, 0, keepdims=False).T * math.sqrt(FF)
    return (grad_hidden, p_basis[None], (q_sum.T / N_REP)[None])


def solution(mesh):
    fine = Mesh(mesh.devices.reshape(N_Y, 2, N_X, N_Z), ("y", "c", "x", "z"))
    rep, exp = ("y", "c"), ("x", "z")
    in_specs = (
        P(rep + exp, None),
        P(rep + exp, None),
        P(rep + exp, None),
        P(rep, exp, None, None),
        P(exp, rep, None),
        P(exp, None, None),
    )
    out_specs = (P(rep + exp, None, None), P(exp, None, None), P(exp, None, None))
    return jax.shard_map(shards, mesh=fine, in_specs=in_specs, out_specs=out_specs, check_vma=False)
```
